32 devices in a mesh: dp: 8 (over y, x, core), tensor: 4 (over z).
Axes of the slice: x: 2, y: 2, z: 4, core: 2. Of those that a mesh axis runs over, the one named last changes fastest.
Arguments:
- tokens: bfloat16 [16384, 1024], P(('dp', 'tensor')), may hold values from -6 to 6
- qkv_weight: bfloat16 [1024, 3, 1024], P('dp', None, 'tensor'), may hold values from -0.1875 to 0.1875
- out_weight: bfloat16 [1024, 1024], P('tensor', 'dp'), may hold values from -3.5 to 3.5
- up_weight: bfloat16 [1024, 4096], P('dp', 'tensor'), may hold values from -0.1875 to 0.1875
- down_weight: bfloat16 [4096, 1024], P('tensor', 'dp'), may hold values from -0.09375 to 0.09375
- mid_gain: float32 [1024], P(('dp', 'tensor')), may hold values from 0.5 to 1.5
- mid_shift: float32 [1024], P(('dp', 'tensor')), may hold values from -3 to 3
- query_bias: float32 [1024], P(('dp', 'tensor')), may hold values from -6 to 6
- value_bias: float32 [1024], P(('dp', 'tensor')), may hold values from -0.75 to 0.75
- out_bias: float32 [1024], P(('dp', 'tensor')), may hold values from -3 to 3
- end_gain: float32 [1024], P(('dp', 'tensor')), may hold values from 0.5 to 1.5
- end_shift: float32 [1024], P(('dp', 'tensor')), may hold values from -3 to 3
- up_bias: float32 [4096], P(('dp', 'tensor')), may hold values from -6 to 6
- down_bias: float32 [1024], P(('dp', 'tensor')), may hold values from -3 to 3
- cotangent: bfloat16 [16384, 1024], P(('dp', 'tensor')), may hold values from -6 to 6
Outputs:
- encoded: bfloat16 [16384, 1024], P(('dp', 'tensor'))
- tokens_grad: float32 [16384, 1024], P(('dp', 'tensor'))
- qkv_grad: float32 [1024, 3, 1024], P('dp', None, 'tensor')
- out_grad: float32 [1024, 1024], P('tensor', 'dp')
- up_grad: float32 [1024, 4096], P('dp', 'tensor')
- down_grad: float32 [4096, 1024], P('tensor', 'dp')
- mid_gain_grad: float32 [1024], P(('dp', 'tensor'))
- mid_shift_grad: float32 [1024], P(('dp', 'tensor'))
- query_bias_grad: float32 [1024], P(('dp', 'tensor'))
- value_bias_grad: float32 [1024], P(('dp', 'tensor'))
- out_bias_grad: float32 [1024], P(('dp', 'tensor'))
- end_gain_grad: float32 [1024], P(('dp', 'tensor'))
- end_shift_grad: float32 [1024], P(('dp', 'tensor'))
- up_bias_grad: float32 [4096], P(('dp', 'tensor'))
- down_bias_grad: float32 [1024], P(('dp', 'tensor'))
The draws below stay inside these ranges and needn't reach their ends.
All inputs are finite; a program needn't handle non-finite values.
Results may differ from the reference program's by a relative error of at most 0.02.
Values may be sent and summed in bfloat16 or wider, within the bound.
No kernel may reach another device: no remote copies, remote signals or barrier semaphores. Data moves between devices by JAX's collectives and lax.ppermute only.
A program may use at most 128 MiB of HBM per device.

```python
import jax
import jax.numpy as jnp
from jax import lax

D = 1024
H = 16
HD = 64
FF = 4096
LEN = 1024
SEQS = 2
TOKENS = 16384


def with_spikes(values, key, source, target, parts, factor):
    owner, partner = [(jnp.arange(values.shape[dim]) // (values.shape[dim] // parts)).reshape([-1 if axis == dim else 1 for axis in range(values.ndim)]) for dim in (source, target)]
    chosen = jax.random.permutation(key, parts)[partner]
    strong = (owner == chosen) | (owner == (partner + parts // 2) % parts)
    return jnp.where(strong, factor * values, values)


def levels(stream_key, shape, shards, smallest, high):
    level = 1.0
    for position, parts in shards:
        draws = jax.random.uniform(jax.random.fold_in(jax.random.fold_in(stream_key, 6), position), (parts,), jnp.float32, smallest / len(shards), high / len(shards))
        level = level * jnp.repeat(jnp.exp(draws), shape[position] // parts).reshape((-1,) + (1,) * (len(shape) - 1 - position))
    return level


def noise(stream_key, shape, spread, bound, cuts=(), kind=jnp.bfloat16):
    result = jax.random.normal(stream_key, shape, jnp.float32) * spread
    if len(cuts) > 0:
        result = levels(stream_key, shape, cuts, -0.22, 0.18) * result
    return jnp.clip(result, min=-bound, max=bound).astype(kind)


def noise_with(stream_key, shape, deviation, reach, cuts, heavy, kind=jnp.bfloat16):
    drawn = deviation * jax.random.normal(stream_key, shape, jnp.float32)
    if cuts:
        drawn = drawn * levels(stream_key, shape, cuts, -0.22, 0.18)
    return jnp.clip(with_spikes(drawn, jax.random.fold_in(stream_key, 3), *heavy), -reach, reach).astype(kind)


def setup_inputs(seed: int = 0) -> dict:
    splits = jax.random.split(jax.random.key(seed), 16)
    return {
        "tokens": noise(splits[0], (TOKENS, D), 1.0, 6.0, ((0, 32),)),
        "qkv_weight": noise(splits[1], (D, 3, D), D ** -0.5, 0.1875, ((0, 8), (2, 4))),
        "out_weight": noise(splits[2], (D, D), (3 * D // LEN) ** -0.5, 3.5, ((0, 4), (1, 8))),
        "up_weight": noise(splits[3], (D, FF), D ** -0.5, 0.1875, ((0, 8), (1, 4))),
        "down_weight": noise(splits[4], (FF, D), FF ** -0.5, 0.09375, ((0, 4), (1, 8))),
        "mid_gain": jnp.clip(1.0 + 0.1 * jax.random.normal(splits[5], (D,), jnp.float32), 0.5, 1.5),
        "mid_shift": noise(splits[6], (D,), 0.2, 3.0, ((0, 32),), jnp.float32),
        "query_bias": noise(splits[7], (D,), 0.5, 6.0, ((0, 32),), jnp.float32),
        "value_bias": noise(splits[8], (D,), 0.05, 0.75, ((0, 32),), jnp.float32),
        "out_bias": noise(splits[9], (D,), 0.2, 3.0, ((0, 32),), jnp.float32),
        "end_gain": jnp.clip(1.0 + 0.1 * jax.random.normal(splits[10], (D,), jnp.float32), 0.5, 1.5),
        "end_shift": noise(splits[11], (D,), 0.2, 3.0, ((0, 32),), jnp.float32),
        "up_bias": noise(splits[12], (FF,), 0.5, 6.0, ((0, 32),), jnp.float32),
        "down_bias": noise(splits[13], (D,), 0.2, 3.0, ((0, 32),), jnp.float32),
        "cotangent": noise_with(splits[14], (TOKENS, D), 1.0, 6.0, ((0, 32),), (0, 1, 32, 2.75)),
    }


@jax.custom_vjp
def low(v):
    return lax.optimization_barrier(v.astype(jnp.bfloat16)).astype(jnp.float32)

@jax.custom_vjp
def low_back(v):
    return v

def low_keep(v):
    return (low(v), None)

def low_pass(kept, grad):
    return (grad,)

def back_keep(v):
    return (v, None)

def back_low(kept, grad):
    return (low(grad),)
low.defvjp(low_keep, low_pass)
low_back.defvjp(back_keep, back_low)
norm_epsilon = 1e-05

def matmul(left, right):
    return jnp.dot(left, right, precision=lax.Precision.HIGHEST, preferred_element_type=jnp.float32)

def normalize(values_in, gain, shift):
    average = lax.optimization_barrier(jnp.mean(values_in, axis=-1, keepdims=True))
    centred = values_in - average
    variance = lax.optimization_barrier(jnp.mean(centred * centred, axis=-1, keepdims=True))
    return centred * lax.rsqrt(variance + norm_epsilon) * gain + shift

def attend(queries, key_rows, value_rows):
    scores = low_back(jnp.einsum('qhd,khd->hqk', queries, key_rows, precision=lax.Precision.HIGHEST) * HD ** (-0.5))
    largest = lax.optimization_barrier(jnp.max(scores, axis=-1, keepdims=True))
    weights = jnp.exp(scores - largest)
    softmax = weights / lax.optimization_barrier(jnp.sum(weights, axis=-1, keepdims=True))
    return jnp.einsum('hqk,khd->qhd', low(softmax), value_rows, precision=lax.Precision.HIGHEST)

def attend_triple(triple):
    return attend(triple[0], triple[1], triple[2])

def encoder(rows_in, qkv_weight, out_weight, up_weight, down_weight, mid_gain, mid_shift, query_bias, value_bias, out_bias, end_gain, end_shift, up_bias, down_bias):
    row_count = rows_in.shape[0]
    joined = matmul(rows_in, qkv_weight.reshape(D, 3 * D)).reshape(row_count, 3, D)
    queries = low(low_back(joined[:, 0] + query_bias))
    key_rows = low(low_back(joined[:, 1]))
    value_rows = low(low_back(joined[:, 2] + value_bias))

    def shaped(t):
        return t.reshape(row_count // LEN, LEN, H, HD)
    context = lax.map(jax.checkpoint(attend_triple), (shaped(queries), shaped(key_rows), shaped(value_rows)))
    context = low(low_back(context.reshape(row_count, D)))
    branch = low_back(matmul(context, out_weight))
    middle = normalize(rows_in + branch + out_bias, mid_gain, mid_shift)
    pre_act = low_back(matmul(low(middle), up_weight) + up_bias)
    hidden = low(jax.nn.gelu(pre_act, approximate=False))
    branch_two = low_back(matmul(hidden, down_weight))
    return normalize(middle + branch_two + down_bias, end_gain, end_shift)

def reference(tokens, qkv_weight, out_weight, up_weight, down_weight, mid_gain, mid_shift, query_bias, value_bias, out_bias, end_gain, end_shift, up_bias, down_bias, cotangent):
    params = tuple((argument.astype(jnp.float32) for argument in (qkv_weight, out_weight, up_weight, down_weight, mid_gain, mid_shift, query_bias, value_bias, out_bias, end_gain, end_shift, up_bias, down_bias)))
    group_rows = SEQS * LEN
    blocks_in = tokens.astype(jnp.float32).reshape(-1, group_rows, D)
    blocks_cot = cotangent.astype(jnp.float32).reshape(-1, group_rows, D)

    def advance(running, inputs):
        rows_in, cot_rows = inputs
        encoded, pullback = jax.vjp(encoder, rows_in, *params)
        gradients = pullback(cot_rows)
        running = tuple((earlier + update for earlier, update in zip(running, gradients[1:])))
        return (running, (encoded.astype(jnp.bfloat16), gradients[0]))
    start_sums = tuple((jnp.zeros_like(argument) for argument in params))
    grad_sums, (encoded, input_grad) = lax.scan(advance, start_sums, (blocks_in, blocks_cot))
    return (encoded.reshape(-1, D), input_grad.reshape(-1, D), grad_sums[0], grad_sums[1], grad_sums[2], grad_sums[3], grad_sums[4], grad_sums[5], grad_sums[6], grad_sums[7], grad_sums[8], grad_sums[9], grad_sums[10], grad_sums[11], grad_sums[12])
```

```python
import functools

import jax
import jax.numpy as jnp
from jax import lax
from jax.experimental import pallas as pl
from jax.experimental.pallas import tpu as pltpu
from jax.sharding import Mesh
from jax.sharding import PartitionSpec as P

HD = 64
LEN = 1024
PAIR = 2 * HD
QB = 256
VMEM = 56 * 1024 * 1024
ALL = ("chip", "core", "tensor")
CHIPS = ("chip", "tensor")
F32 = jnp.float32
BF16 = jnp.bfloat16
SCALE = HD ** (-0.5)
EPS = 1e-05


def nt(left, right):
    return lax.dot_general(left, right, (((1,), (1,)), ((), ())), preferred_element_type=F32)


def nn(left, right):
    return lax.dot_general(left, right, (((1,), (0,)), ((), ())), preferred_element_type=F32)


def tn(left, right):
    return lax.dot_general(left, right, (((0,), (0,)), ((), ())), preferred_element_type=F32)


def head_lane(rows, head):
    lane = lax.broadcasted_iota(jnp.int32, (rows, PAIR), 1)
    return (lane >= head * HD) & (lane < (head + 1) * HD)


def attend_kernel(q_ref, k_ref, v_ref, o_ref, lse_ref):
    rows = q_ref.shape[0]
    keys = k_ref[...]
    values_t = v_ref[...].astype(F32).T
    sub = lax.broadcasted_iota(jnp.int32, values_t.shape, 0)
    values_h = [
        jnp.where((sub >= h * HD) & (sub < (h + 1) * HD), values_t, 1.0).astype(BF16)
        for h in range(2)
    ]

    def block(step, carry):
        at = pl.ds(pl.multiple_of(step * QB, QB), QB)
        q = q_ref[at, :].astype(F32) * SCALE
        parts = []
        for h in range(2):
            qm = jnp.where(head_lane(QB, h), q, 0.0).astype(BF16)
            scores = nt(keys, qm)
            largest = jnp.max(scores, axis=0, keepdims=True)
            weights = jnp.exp(scores - largest).astype(BF16)
            out = nn(values_h[h], weights)
            total = out[(1 - h) * HD : (1 - h) * HD + 1, :]
            parts.append(out[h * HD : (h + 1) * HD, :] / total)
            lse_ref[0, h : h + 1, at] = largest + jnp.log(total)
        o_ref[at, :] = jnp.concatenate(parts, axis=0).T.astype(BF16)
        return carry

    lax.fori_loop(0, rows // QB, block, 0)


def attend(joint, groups):
    rows = joint.shape[0]
    part = lambda c: pl.BlockSpec((rows, PAIR), lambda z: (0, 3 * z + c))
    return pl.pallas_call(
        attend_kernel,
        grid=(groups,),
        in_specs=[part(0), part(1), part(2)],
        out_specs=[
            pl.BlockSpec((rows, PAIR), lambda z: (0, z)),
            pl.BlockSpec((1, 2, rows), lambda z: (z, 0, 0)),
        ],
        out_shape=[
            jax.ShapeDtypeStruct((rows, groups * PAIR), BF16),
            jax.ShapeDtypeStruct((groups, 2, rows), F32),
        ],
        compiler_params=pltpu.CompilerParams(vmem_limit_bytes=VMEM),
        cost_estimate=pl.CostEstimate(
            flops=groups * 2 * 16 * rows * rows * HD,
            bytes_accessed=groups * rows * PAIR * 8,
            transcendentals=groups * 2 * rows * rows,
        ),
        name="attend",
    )(joint, joint, joint)


def attend_back_kernel(q_ref, k_ref, v_ref, g_ref, o_ref, lse_ref, d_ref, sum_ref, dk_ref, dv_ref):
    rows = q_ref.shape[0]
    keys = k_ref[...]
    values = v_ref[...]
    keys_t = keys.astype(F32).T
    sub = lax.broadcasted_iota(jnp.int32, keys_t.shape, 0)
    keys_h = [
        jnp.where((sub >= h * HD) & (sub < (h + 1) * HD), keys_t, 0.0).astype(BF16)
        for h in range(2)
    ]
    dk_ref[...] = jnp.zeros_like(dk_ref)
    dv_ref[...] = jnp.zeros_like(dv_ref)

    def block(step, query_sum):
        at = pl.ds(pl.multiple_of(step * QB, QB), QB)
        q = q_ref[at, :].astype(F32) * SCALE
        g = g_ref[at, :].astype(F32)
        inner = (g * o_ref[at, :].astype(F32)).T
        dq = None
        for h in range(2):
            here = head_lane(QB, h)
            qm = jnp.where(here, q, 0.0).astype(BF16)
            gm = jnp.where(here, g, 0.0).astype(BF16)
            delta = jnp.sum(inner[h * HD : (h + 1) * HD, :], axis=0, keepdims=True)
            probs = jnp.exp(nt(keys, qm) - lse_ref[0, h : h + 1, at])
            score_grad = (probs * (nt(values, gm) - delta)).astype(BF16)
            dv_ref[...] += nn(probs.astype(BF16), gm)
            dk_ref[...] += nn(score_grad, qm)
            part = nn(keys_h[h], score_grad)
            dq = part if dq is None else dq + part
        dq = (dq.T * SCALE).astype(BF16)
        d_ref[at, 0:PAIR] = dq
        return query_sum + jnp.sum(dq.astype(F32), axis=0, keepdims=True)

    query_sum = lax.fori_loop(0, rows // QB, block, jnp.zeros((1, PAIR), F32))
    dv = dv_ref[...].astype(BF16)
    d_ref[:, PAIR : 2 * PAIR] = dk_ref[...].astype(BF16)
    d_ref[:, 2 * PAIR :] = dv
    sum_ref[0, 0:1, :] = query_sum
    sum_ref[0, 1:2, :] = jnp.sum(dv.astype(F32), axis=0, keepdims=True)


def attend_back(joint, context_grad, context, lse, groups):
    rows = joint.shape[0]
    part = lambda c: pl.BlockSpec((rows, PAIR), lambda z: (0, 3 * z + c))
    one = pl.BlockSpec((rows, PAIR), lambda z: (0, z))
    return pl.pallas_call(
        attend_back_kernel,
        grid=(groups,),
        in_specs=[
            part(0),
            part(1),
            part(2),
            one,
            one,
            pl.BlockSpec((1, 2, rows), lambda z: (z, 0, 0)),
        ],
        out_specs=[
            pl.BlockSpec((rows, 3 * PAIR), lambda z: (0, z)),
            pl.BlockSpec((1, 2, PAIR), lambda z: (z, 0, 0)),
        ],
        out_shape=[
            jax.ShapeDtypeStruct((rows, 3 * groups * PAIR), BF16),
            jax.ShapeDtypeStruct((groups, 2, PAIR), F32),
        ],
        scratch_shapes=[pltpu.VMEM((rows, PAIR), F32), pltpu.VMEM((rows, PAIR), F32)],
        compiler_params=pltpu.CompilerParams(vmem_limit_bytes=VMEM),
        cost_estimate=pl.CostEstimate(
            flops=groups * 2 * 40 * rows * rows * HD,
            bytes_accessed=groups * rows * PAIR * 16,
            transcendentals=groups * 2 * rows * rows,
        ),
        name="attend_back",
    )(joint, joint, joint, context_grad, context, lse)


def normalized(values_in):
    average = jnp.mean(values_in, axis=-1, keepdims=True)
    centred = values_in - average
    inverse = lax.rsqrt(jnp.mean(centred * centred, axis=-1, keepdims=True) + EPS)
    return centred * inverse, inverse


def norm_back(grad, unit, inverse, gain):
    gain_part = jnp.sum(grad * unit, axis=0)
    shift_part = jnp.sum(grad, axis=0)
    u = grad * gain
    back = inverse * (
        u
        - jnp.mean(u, axis=-1, keepdims=True)
        - unit * jnp.mean(u * unit, axis=-1, keepdims=True)
    )
    return back, gain_part, shift_part, jnp.sum(back, axis=0)


def gelu_pair(x):
    phi = 0.5 * (1.0 + lax.erf(x * (0.5**0.5)))
    slope = phi + x * jnp.exp(-0.5 * x * x) * (0.5 / jnp.pi) ** 0.5
    return (x * phi).astype(BF16), slope.astype(BF16)


def to_other(value):
    return lax.ppermute(value, "core", [(0, 1), (1, 0)])


def both_rows(value):
    return jnp.concatenate((value, to_other(value)), axis=0)


def summed_rows(rows, weight, dot):
    half = rows.shape[0] // 2
    away = to_other(dot(rows[half:], weight).astype(BF16))
    return dot(rows[:half], weight) + away.astype(F32)


def on_device(
    tokens,
    qkv_weight,
    out_weight,
    up_weight,
    down_weight,
    mid_gain,
    mid_shift,
    query_bias,
    value_bias,
    out_bias,
    end_gain,
    end_shift,
    up_bias,
    down_bias,
    cotangent,
):
    core = lax.axis_index("core")
    n_chip = lax.axis_size("chip")
    n_ten = lax.axis_size("tensor")
    strip = tokens.shape[0]
    width = tokens.shape[1]
    slab = qkv_weight.shape[0]
    cols = qkv_weight.shape[2] // 2
    units = up_weight.shape[1] // 2
    assert 2 * strip == LEN and cols == PAIR

    pairs = []
    for z in range(n_ten):
        pairs.append((z, z) if z % 2 == 0 else (z, n_ten + z - 1))
        pairs.append((n_ten + z, z + 1) if z % 2 == 0 else (n_ten + z, n_ten + z))
    swap = lambda value: lax.ppermute(value, ("core", "tensor"), pairs)

    vectors = (
        mid_gain,
        mid_shift,
        query_bias,
        value_bias,
        out_bias,
        end_gain,
        end_shift,
        up_bias,
        down_bias,
    )
    packed = lax.all_gather(jnp.concatenate(vectors), ALL, axis=0, tiled=False)
    sizes = [v.shape[0] for v in vectors]
    starts = [sum(sizes[:i]) for i in range(len(sizes))]
    whole = [packed[:, s : s + n].reshape(-1) for s, n in zip(starts, sizes)]
    gain_mid, shift_mid, bias_q, bias_v, bias_out, gain_end, shift_end, bias_up, bias_down = whole

    def own_half(vector):
        return lax.dynamic_index_in_dim(vector.reshape(n_ten, 2, -1), core, 1, keepdims=False)

    bias_q, bias_v, bias_up = own_half(bias_q), own_half(bias_v), own_half(bias_up)
    bias_qkv = jnp.stack((bias_q, jnp.zeros_like(bias_q), bias_v), axis=1).reshape(-1)
    bias_up = bias_up.reshape(-1)

    stack = jnp.concatenate(
        (
            jnp.moveaxis(qkv_weight.reshape(slab, 3, 2, cols), 0, 3)
            .transpose(1, 0, 2, 3)
            .reshape(2, 3 * cols, slab),
            out_weight.reshape(2, cols, slab),
            up_weight.T.reshape(2, units, slab),
            down_weight.reshape(2, units, slab),
        ),
        axis=1,
    )
    keep = lax.dynamic_index_in_dim(stack, core, 0, keepdims=False)
    came = to_other(lax.dynamic_index_in_dim(stack, 1 - core, 0, keepdims=False))
    shard = jnp.concatenate(
        (jnp.where(core == 0, keep, came), jnp.where(core == 0, came, keep)), axis=1
    )
    bounds = (0, 3 * cols, 4 * cols, 4 * cols + units, 4 * cols + 2 * units)

    def gathered(index):
        part = shard[bounds[index] : bounds[index + 1]]
        rows = part.shape[0]
        full = lax.all_gather(part, CHIPS, axis=0, tiled=False)
        return (
            full.reshape(n_chip, n_ten, rows, 2 * slab)
            .transpose(1, 2, 0, 3)
            .reshape(n_ten * rows, width)
        )

    w_qkv, w_out, w_up, w_down = (gathered(i) for i in range(4))

    mine = swap(tokens)
    cot = swap(cotangent)
    seen = both_rows(mine)

    joint = (nt(seen, w_qkv) + bias_qkv).astype(BF16)
    context, lse = attend(joint, n_ten)
    branch = summed_rows(context, w_out, nn)
    unit_mid, inverse_mid = normalized(mine.astype(F32) + branch + bias_out)
    middle = unit_mid * gain_mid + shift_mid
    seen_middle = both_rows(middle.astype(BF16))
    hidden, slope = gelu_pair(nt(seen_middle, w_up) + bias_up)
    branch_two = summed_rows(hidden, w_down, nn)
    unit_end, inverse_end = normalized(middle + branch_two + bias_down)
    encoded = swap((unit_end * gain_end + shift_end).astype(BF16))

    second_grad, end_gain_part, end_shift_part, down_bias_part = norm_back(
        cot.astype(F32), unit_end, inverse_end, gain_end
    )
    seen_second = both_rows(second_grad.astype(BF16))
    pre_grad = (nt(seen_second, w_down) * slope.astype(F32)).astype(BF16)
    up_bias_part = jnp.sum(pre_grad.astype(F32), axis=0)
    middle_grad = summed_rows(pre_grad, w_up, nn) + second_grad
    down_sum = tn(hidden, seen_second)
    up_sum = tn(pre_grad, seen_middle)
    first_grad, mid_gain_part, mid_shift_part, out_bias_part = norm_back(
        middle_grad, unit_mid, inverse_mid, gain_mid
    )
    seen_first = both_rows(first_grad.astype(BF16))
    context_grad = nt(seen_first, w_out).astype(BF16)
    out_sum = tn(context, seen_first)
    qkv_low, bias_sums = attend_back(joint, context_grad, context, lse, n_ten)
    qkv_sum = tn(qkv_low, seen)
    input_grad = summed_rows(qkv_low, w_qkv, nn) + first_grad
    input_grad = swap(input_grad.astype(BF16)).astype(F32)

    def scattered(total, extra=None):
        rows = total.shape[0] // n_ten
        blocks = (
            total.astype(BF16)
            .reshape(n_ten, rows, n_chip, 2 * slab)
            .transpose(2, 0, 1, 3)
            .reshape(n_chip * n_ten, rows, 2 * slab)
        )
        if extra is not None:
            blocks = jnp.concatenate((blocks, extra), axis=1)
        return lax.psum_scatter(blocks, CHIPS, scatter_dimension=0, tiled=False)

    wide = (
        mid_gain_part,
        mid_shift_part,
        out_bias_part,
        end_gain_part,
        end_shift_part,
        down_bias_part,
    )
    narrow = (bias_sums[:, 0], bias_sums[:, 1], up_bias_part)
    aligned = n_chip == n_ten
    extra = None
    if aligned:
        tail = []
        for vector in wide:
            tail.append(vector.reshape(n_chip, 2, n_ten, -1).transpose(0, 2, 1, 3))
        for vector in narrow:
            tail.append(vector.reshape(n_chip, n_ten, 1, -1))
        tail = [t.reshape(n_chip * n_ten, -1) for t in tail]
        tail_sizes = [t.shape[1] for t in tail]
        used = sum(tail_sizes)
        lines = -(-used // (2 * slab))
        lines = -(-lines // 16) * 16
        extra = jnp.concatenate(
            tail + [jnp.zeros((n_chip * n_ten, lines * 2 * slab - used), F32)], axis=1
        )
        extra = extra.reshape(n_chip * n_ten, lines, 2 * slab).astype(BF16)
    down_part = scattered(down_sum)
    up_part = scattered(up_sum)
    out_part = scattered(out_sum)
    qkv_part = scattered(qkv_sum, extra)
    if aligned:
        vector_line = qkv_part[3 * cols :].reshape(-1).astype(F32)
        qkv_part = qkv_part[: 3 * cols]
    parts = jnp.concatenate((qkv_part, out_part, up_part, down_part), axis=0)
    parts = parts.reshape(-1, 2, slab)
    keep = lax.dynamic_index_in_dim(parts, core, 1, keepdims=False)
    came = to_other(lax.dynamic_index_in_dim(parts, 1 - core, 1, keepdims=False))
    halves = jnp.stack(
        (jnp.where(core == 0, keep, came), jnp.where(core == 0, came, keep)), axis=0
    ).astype(F32)
    cut = [halves[:, bounds[i] : bounds[i + 1]] for i in range(4)]
    qkv_out = (
        cut[0].reshape(2, 3, cols, slab).transpose(3, 1, 0, 2).reshape(slab, 3, 2 * cols)
    )
    out_out = cut[1].reshape(2 * cols, slab)
    up_out = cut[2].reshape(2 * units, slab).T
    down_out = cut[3].reshape(2 * units, slab)

    if aligned:
        n_wide = sum(tail_sizes[:6])
        doubled = vector_line[:n_wide].reshape(6, 2, -1)
        own = lax.dynamic_index_in_dim(doubled, core, 1, keepdims=False)
        away = to_other(lax.dynamic_index_in_dim(doubled, 1 - core, 1, keepdims=False))
        own = own + away
        rest = vector_line[n_wide:]
        n_q, n_v, n_up = tail_sizes[6:]
        grads = [own[i] for i in range(6)] + [
            rest[:n_q],
            rest[n_q : n_q + n_v],
            rest[n_q + n_v : n_q + n_v + n_up],
        ]
    else:

        def placed(vector):
            blank = jnp.zeros((n_ten, 2, vector.size // n_ten), F32)
            return lax.dynamic_update_slice_in_dim(
                blank, vector.reshape(n_ten, 1, -1), core, 1
            ).reshape(-1)

        flat = list(wide) + [placed(v) for v in narrow]
        devices = n_chip * 2 * n_ten
        flat = [v.reshape(devices, -1) for v in flat]
        sums = lax.psum_scatter(
            jnp.concatenate(flat, axis=1), ALL, scatter_dimension=0, tiled=False
        )
        grads = []
        at = 0
        for v in flat:
            grads.append(sums[at : at + v.shape[1]])
            at += v.shape[1]
    g_mid_gain, g_mid_shift, g_out_bias, g_end_gain, g_end_shift, g_down_bias, g_q, g_v, g_up = (
        grads
    )
    return (
        encoded,
        input_grad,
        qkv_out,
        out_out,
        up_out,
        down_out,
        g_mid_gain,
        g_mid_shift,
        g_q,
        g_v,
        g_out_bias,
        g_end_gain,
        g_end_shift,
        g_up,
        g_down_bias,
    )


def solution(mesh):
    n_dp, n_ten = mesh.devices.shape
    inner = Mesh(mesh.devices.reshape(n_dp // 2, 2, n_ten), ALL)
    rows = P(ALL, None)
    vector = P(ALL)
    dp = ("chip", "core")
    weights = (P(dp, None, "tensor"), P("tensor", dp), P(dp, "tensor"), P("tensor", dp))
    return jax.shard_map(
        on_device,
        mesh=inner,
        in_specs=(rows, *weights, *(vector,) * 9, rows),
        out_specs=(rows, rows, *weights, *(vector,) * 9),
        check_vma=False,
    )
```

```python
import functools

import jax
import jax.numpy as jnp
from jax import lax
from jax.experimental import pallas as pl
from jax.experimental.pallas import tpu as pltpu
from jax.sharding import Mesh
from jax.sharding import PartitionSpec as P

HD = 64
LEN = 1024
PAIR = 2 * HD
QB = 256
VMEM = 56 * 1024 * 1024
ALL = ("chip", "core", "tensor")
CHIPS = ("chip", "tensor")
F32 = jnp.float32
BF16 = jnp.bfloat16
SCALE = HD ** (-0.5)
EPS = 1e-05


def nt(left, right):
    return lax.dot_general(left, right, (((1,), (1,)), ((), ())), preferred_element_type=F32)


def nn(left, right):
    return lax.dot_general(left, right, (((1,), (0,)), ((), ())), preferred_element_type=F32)


def tn(left, right):
    return lax.dot_general(left, right, (((0,), (0,)), ((), ())), preferred_element_type=F32)


def head_lane(rows, head):
    lane = lax.broadcasted_iota(jnp.int32, (rows, PAIR), 1)
    return (lane >= head * HD) & (lane < (head + 1) * HD)


def attend_kernel(q_ref, k_ref, v_ref, o_ref, lse_ref):
    rows = q_ref.shape[0]
    keys = k_ref[...]
    values_t = v_ref[...].astype(F32).T
    sub = lax.broadcasted_iota(jnp.int32, values_t.shape, 0)
    values_h = [
        jnp.where((sub >= h * HD) & (sub < (h + 1) * HD), values_t, 1.0).astype(BF16)
        for h in range(2)
    ]

    def block(step, carry):
        at = pl.ds(pl.multiple_of(step * QB, QB), QB)
        q = q_ref[at, :].astype(F32) * SCALE
        parts = []
        for h in range(2):
            qm = jnp.where(head_lane(QB, h), q, 0.0).astype(BF16)
            scores = nt(keys, qm)
            largest = jnp.max(scores, axis=0, keepdims=True)
            weights = jnp.exp(scores - largest).astype(BF16)
            out = nn(values_h[h], weights)
            total = out[(1 - h) * HD : (1 - h) * HD + 1, :]
            parts.append(out[h * HD : (h + 1) * HD, :] / total)
            lse_ref[0, h : h + 1, at] = largest + jnp.log(total)
        o_ref[at, :] = jnp.concatenate(parts, axis=0).T.astype(BF16)
        return carry

    lax.fori_loop(0, rows // QB, block, 0)


def attend(joint, groups):
    rows = joint.shape[0]
    part = lambda c: pl.BlockSpec((rows, PAIR), lambda z: (0, 3 * z + c))
    return pl.pallas_call(
        attend_kernel,
        grid=(groups,),
        in_specs=[part(0), part(1), part(2)],
        out_specs=[
            pl.BlockSpec((rows, PAIR), lambda z: (0, z)),
            pl.BlockSpec((1, 2, rows), lambda z: (z, 0, 0)),
        ],
        out_shape=[
            jax.ShapeDtypeStruct((rows, groups * PAIR), BF16),
            jax.ShapeDtypeStruct((groups, 2, rows), F32),
        ],
        compiler_params=pltpu.CompilerParams(vmem_limit_bytes=VMEM),
        cost_estimate=pl.CostEstimate(
            flops=groups * 2 * 16 * rows * rows * HD,
            bytes_accessed=groups * rows * PAIR * 8,
            transcendentals=groups * 2 * rows * rows,
        ),
        name="attend",
    )(joint, joint, joint)


def attend_back_kernel(q_ref, k_ref, v_ref, g_ref, o_ref, lse_ref, d_ref, sum_ref, dk_ref, dv_ref):
    rows = q_ref.shape[0]
    keys = k_ref[...]
    values = v_ref[...]
    keys_t = keys.astype(F32).T
    sub = lax.broadcasted_iota(jnp.int32, keys_t.shape, 0)
    keys_h = [
        jnp.where((sub >= h * HD) & (sub < (h + 1) * HD), keys_t, 0.0).astype(BF16)
        for h in range(2)
    ]
    dk_ref[...] = jnp.zeros_like(dk_ref)
    dv_ref[...] = jnp.zeros_like(dv_ref)

    def block(step, query_sum):
        at = pl.ds(pl.multiple_of(step * QB, QB), QB)
        q = q_ref[at, :].astype(F32) * SCALE
        g = g_ref[at, :].astype(F32)
        inner = (g * o_ref[at, :].astype(F32)).T
        dq = None
        for h in range(2):
            here = head_lane(QB, h)
            qm = jnp.where(here, q, 0.0).astype(BF16)
            gm = jnp.where(here, g, 0.0).astype(BF16)
            delta = jnp.sum(inner[h * HD : (h + 1) * HD, :], axis=0, keepdims=True)
            probs = jnp.exp(nt(keys, qm) - lse_ref[0, h : h + 1, at])
            score_grad = (probs * (nt(values, gm) - delta)).astype(BF16)
            dv_ref[...] += nn(probs.astype(BF16), gm)
            dk_ref[...] += nn(score_grad, qm)
            part = nn(keys_h[h], score_grad)
            dq = part if dq is None else dq + part
        dq = (dq.T * SCALE).astype(BF16)
        d_ref[at, 0:PAIR] = dq
        return query_sum + jnp.sum(dq.astype(F32), axis=0, keepdims=True)

    query_sum = lax.fori_loop(0, rows // QB, block, jnp.zeros((1, PAIR), F32))
    dv = dv_ref[...].astype(BF16)
    d_ref[:, PAIR : 2 * PAIR] = dk_ref[...].astype(BF16)
    d_ref[:, 2 * PAIR :] = dv
    sum_ref[0, 0:1, :] = query_sum
    sum_ref[0, 1:2, :] = jnp.sum(dv.astype(F32), axis=0, keepdims=True)


def attend_back(joint, context_grad, context, lse, groups):
    rows = joint.shape[0]
    part = lambda c: pl.BlockSpec((rows, PAIR), lambda z: (0, 3 * z + c))
    one = pl.BlockSpec((rows, PAIR), lambda z: (0, z))
    return pl.pallas_call(
        attend_back_kernel,
        grid=(groups,),
        in_specs=[
            part(0),
            part(1),
            part(2),
            one,
            one,
            pl.BlockSpec((1, 2, rows), lambda z: (z, 0, 0)),
        ],
        out_specs=[
            pl.BlockSpec((rows, 3 * PAIR), lambda z: (0, z)),
            pl.BlockSpec((1, 2, PAIR), lambda z: (z, 0, 0)),
        ],
        out_shape=[
            jax.ShapeDtypeStruct((rows, 3 * groups * PAIR), BF16),
            jax.ShapeDtypeStruct((groups, 2, PAIR), F32),
        ],
        scratch_shapes=[pltpu.VMEM((rows, PAIR), F32), pltpu.VMEM((rows, PAIR), F32)],
        compiler_params=pltpu.CompilerParams(vmem_limit_bytes=VMEM),
        cost_estimate=pl.CostEstimate(
            flops=groups * 2 * 40 * rows * rows * HD,
            bytes_accessed=groups * rows * PAIR * 16,
            transcendentals=groups * 2 * rows * rows,
        ),
        name="attend_back",
    )(joint, joint, joint, context_grad, context, lse)


def normalized(values_in):
    average = jnp.mean(values_in, axis=-1, keepdims=True)
    centred = values_in - average
    inverse = lax.rsqrt(jnp.mean(centred * centred, axis=-1, keepdims=True) + EPS)
    return centred * inverse, inverse


def norm_back(grad, unit, inverse, gain):
    gain_part = jnp.sum(grad * unit, axis=0)
    shift_part = jnp.sum(grad, axis=0)
    u = grad * gain
    back = inverse * (
        u
        - jnp.mean(u, axis=-1, keepdims=True)
        - unit * jnp.mean(u * unit, axis=-1, keepdims=True)
    )
    return back, gain_part, shift_part, jnp.sum(back, axis=0)


def gelu_pair(x):
    phi = 0.5 * (1.0 + lax.erf(x * (0.5**0.5)))
    slope = phi + x * jnp.exp(-0.5 * x * x) * (0.5 / jnp.pi) ** 0.5
    return (x * phi).astype(BF16), slope.astype(BF16)


def to_other(value):
    return lax.ppermute(value, "core", [(0, 1), (1, 0)])


def both_rows(value):
    return jnp.concatenate((value, to_other(value)), axis=0)


def summed_rows(rows, weight, dot):
    half = rows.shape[0] // 2
    away = to_other(dot(rows[half:], weight).astype(BF16))
    return dot(rows[:half], weight) + away.astype(F32)


def assemble_kernel(chip_ref, own_ref, x_ref, y_ref, low_ref, high_ref, *out_refs):
    chip = chip_ref[0]
    wide = own_ref.shape[2]
    lower = pl.program_id(0) < pl.num_programs(0) // 2
    start = 0
    for out_ref in out_refs:
        rows = slice(start, start + out_ref.shape[1])
        start += out_ref.shape[1]

        def columns(move):
            at = pl.multiple_of(lax.bitwise_xor(chip, move) * wide, wide)
            return pl.ds(at, wide)

        out_ref[0, :, columns(0)] = own_ref[0, rows, :]
        out_ref[0, :, columns(1)] = x_ref[0, rows, :]
        out_ref[0, :, columns(2)] = y_ref[0, rows, :]
        far = jnp.where(lower, low_ref[0, rows, :], high_ref[0, rows, :])
        out_ref[0, :, columns(3)] = far


def assemble(chip, blocks, heights):
    own, low = blocks[0], blocks[3]
    members, rows, wide = own.shape
    half = low.shape[0]
    one = pl.BlockSpec((1, rows, wide), lambda z, c: (z, 0, 0))
    return pl.pallas_call(
        assemble_kernel,
        grid_spec=pltpu.PrefetchScalarGridSpec(
            num_scalar_prefetch=1,
            grid=(members,),
            in_specs=[
                one,
                one,
                one,
                pl.BlockSpec((1, rows, wide), lambda z, c: (jnp.minimum(z, half - 1), 0, 0)),
                pl.BlockSpec((1, rows, wide), lambda z, c: (jnp.maximum(z - half, 0), 0, 0)),
            ],
            out_specs=[pl.BlockSpec((1, h, 4 * wide), lambda z, c: (z, 0, 0)) for h in heights],
        ),
        out_shape=[jax.ShapeDtypeStruct((members, h, 4 * wide), BF16) for h in heights],
        compiler_params=pltpu.CompilerParams(vmem_limit_bytes=VMEM),
        cost_estimate=pl.CostEstimate(
            flops=0, bytes_accessed=16 * members * rows * wide, transcendentals=0
        ),
        name="assemble",
    )(chip.reshape(1), *blocks)


def to_chip(value, move):
    return lax.ppermute(value, "chip", [(i, i ^ move) for i in range(4)])


def after(value, *earlier):
    return lax.optimization_barrier((value, *earlier))[0]


def layer_gather(part):
    own = lax.all_gather(part, "tensor", axis=0, tiled=False)
    half = own.shape[0] // 2
    by_x = to_chip(own, 1)
    by_y = to_chip(own, 2)
    return own, by_x, by_y, to_chip(by_y[:half], 1), to_chip(by_x[half:], 2)


def layer_scatter(block):
    far = block(3)
    half = far.shape[0] // 2
    low = to_chip(far[:half], 1)
    high = to_chip(far[half:], 2)
    near_x = block(1)
    near_y = block(2)
    add = lambda a, b: (a.astype(F32) + b.astype(F32)).astype(BF16)
    near_y = jnp.concatenate((add(near_y[:half], low), near_y[half:]), axis=0)
    near_x = jnp.concatenate((near_x[:half], add(near_x[half:], high)), axis=0)
    came_y = to_chip(near_y, 2)
    came_x = to_chip(near_x, 1)
    own = block(0)
    return (own.astype(F32) + came_x.astype(F32) + came_y.astype(F32)).astype(BF16)


def in_chip_order(chip, blocks):
    b0, b1, b2, b3 = blocks
    odd_x = (chip & 1) == 1
    odd_y = (chip & 2) == 2
    a0, a1 = jnp.where(odd_x, b1, b0), jnp.where(odd_x, b0, b1)
    a2, a3 = jnp.where(odd_x, b3, b2), jnp.where(odd_x, b2, b3)
    return jnp.stack(
        (
            jnp.where(odd_y, a2, a0),
            jnp.where(odd_y, a3, a1),
            jnp.where(odd_y, a0, a2),
            jnp.where(odd_y, a1, a3),
        )
    )


def on_device(
    tokens,
    qkv_weight,
    out_weight,
    up_weight,
    down_weight,
    mid_gain,
    mid_shift,
    query_bias,
    value_bias,
    out_bias,
    end_gain,
    end_shift,
    up_bias,
    down_bias,
    cotangent,
):
    core = lax.axis_index("core")
    chip = lax.axis_index("chip")
    n_chip = lax.axis_size("chip")
    n_ten = lax.axis_size("tensor")
    strip = tokens.shape[0]
    width = tokens.shape[1]
    slab = qkv_weight.shape[0]
    cols = qkv_weight.shape[2] // 2
    units = up_weight.shape[1] // 2
    assert 2 * strip == LEN and cols == PAIR

    pairs = []
    for z in range(n_ten):
        pairs.append((z, z) if z % 2 == 0 else (z, n_ten + z - 1))
        pairs.append((n_ten + z, z + 1) if z % 2 == 0 else (n_ten + z, n_ten + z))
    swap = lambda value: lax.ppermute(value, ("core", "tensor"), pairs)

    vectors = (
        mid_gain,
        mid_shift,
        query_bias,
        value_bias,
        out_bias,
        end_gain,
        end_shift,
        up_bias,
        down_bias,
    )
    stack = jnp.concatenate(
        (
            jnp.moveaxis(qkv_weight.reshape(slab, 3, 2, cols), 0, 3)
            .transpose(1, 0, 2, 3)
            .reshape(2, 3 * cols, slab),
            out_weight.reshape(2, cols, slab),
            up_weight.T.reshape(2, units, slab),
            down_weight.reshape(2, units, slab),
        ),
        axis=1,
    )
    keep = lax.dynamic_index_in_dim(stack, core, 0, keepdims=False)
    came = to_other(lax.dynamic_index_in_dim(stack, 1 - core, 0, keepdims=False))
    shard = jnp.concatenate(
        (jnp.where(core == 0, keep, came), jnp.where(core == 0, came, keep)), axis=1
    )
    bounds = (0, 3 * cols, 4 * cols, 4 * cols + units, 4 * cols + 2 * units)

    mine = swap(tokens)
    seen = both_rows(mine)
    sizes = [v.shape[0] for v in vectors]
    n_vec = sum(sizes)
    flat = jnp.concatenate(vectors)
    small = n_chip == 4 and n_ten == 4
    if small:
        coarse = lax.reduce_precision(flat, 8, 7)
        middle_bits = lax.reduce_precision(flat - coarse, 8, 7)
        thirds = jnp.concatenate((coarse, middle_bits, flat - coarse - middle_bits)).astype(BF16)
        came = to_other(thirds)
        both = jnp.concatenate(
            (jnp.where(core == 0, thirds, came), jnp.where(core == 0, came, thirds))
        )
        lines = -(-both.size // (16 * 2 * slab)) * 16
        both = jnp.concatenate((both, jnp.zeros((lines * 2 * slab - both.size,), BF16)))
        first = jnp.concatenate((shard[: bounds[1]], both.reshape(lines, 2 * slab)), axis=0)
        blocks = layer_gather(first)
        (w_qkv,) = assemble(chip, blocks, (3 * cols,))
        tails = [b[:, 3 * cols :] for b in blocks]
        tails = tails[:3] + [jnp.concatenate(tails[3:], axis=0)]
        packed = in_chip_order(chip, tails).reshape(n_chip, n_ten, -1)[:, :, : 6 * n_vec]
        packed = packed.reshape(n_chip, n_ten, 2, 3, n_vec).astype(F32)
        packed = packed[:, :, :, 0] + packed[:, :, :, 1] + packed[:, :, :, 2]
        packed = packed.transpose(0, 2, 1, 3).reshape(-1, n_vec)
        second = after(shard[bounds[1] : bounds[3]], blocks[0])
        blocks = layer_gather(second)
        w_out, w_up = assemble(chip, blocks, (cols, units))
        third = after(shard[bounds[3] :], blocks[0])
        blocks = layer_gather(third)
        (w_down,) = assemble(chip, blocks, (units,))
        w_qkv, w_out, w_up, w_down = (w.reshape(-1, width) for w in (w_qkv, w_out, w_up, w_down))
    else:

        def gathered(index):
            part = shard[bounds[index] : bounds[index + 1]]
            rows = part.shape[0]
            full = lax.all_gather(part, CHIPS, axis=0, tiled=False)
            return (
                full.reshape(n_chip, n_ten, rows, 2 * slab)
                .transpose(1, 2, 0, 3)
                .reshape(n_ten * rows, width)
            )

        w_qkv, w_out, w_up, w_down = (gathered(i) for i in range(4))
        packed = lax.all_gather(flat, ALL, axis=0, tiled=False)
    starts = [sum(sizes[:i]) for i in range(len(sizes))]
    whole = [packed[:, s : s + n].reshape(-1) for s, n in zip(starts, sizes)]
    gain_mid, shift_mid, bias_q, bias_v, bias_out, gain_end, shift_end, bias_up, bias_down = whole

    def own_half(vector):
        return lax.dynamic_index_in_dim(vector.reshape(n_ten, 2, -1), core, 1, keepdims=False)

    bias_q, bias_v, bias_up = own_half(bias_q), own_half(bias_v), own_half(bias_up)
    bias_qkv = jnp.stack((bias_q, jnp.zeros_like(bias_q), bias_v), axis=1).reshape(-1)
    bias_up = bias_up.reshape(-1)

    joint = (nt(seen, w_qkv) + bias_qkv).astype(BF16)
    cot = swap(after(cotangent, joint))
    context, lse = attend(joint, n_ten)
    branch = summed_rows(context, w_out, nn)
    unit_mid, inverse_mid = normalized(mine.astype(F32) + branch + bias_out)
    middle = unit_mid * gain_mid + shift_mid
    seen_middle = both_rows(middle.astype(BF16))
    hidden, slope = gelu_pair(nt(seen_middle, w_up) + bias_up)
    branch_two = summed_rows(hidden, w_down, nn)
    unit_end, inverse_end = normalized(middle + branch_two + bias_down)
    encoded = swap((unit_end * gain_end + shift_end).astype(BF16))

    second_grad, end_gain_part, end_shift_part, down_bias_part = norm_back(
        cot.astype(F32), unit_end, inverse_end, gain_end
    )
    seen_second = both_rows(second_grad.astype(BF16))
    pre_grad = (nt(seen_second, w_down) * slope.astype(F32)).astype(BF16)
    up_bias_part = jnp.sum(pre_grad.astype(F32), axis=0)
    middle_grad = summed_rows(pre_grad, w_up, nn) + second_grad

    def beside(rows, columns):
        def block(move):
            at = lax.bitwise_xor(chip, move) * (2 * slab)
            return tn(rows, lax.dynamic_slice_in_dim(columns, at, 2 * slab, axis=1)).astype(BF16)

        return block

    if small:
        down_layer = layer_scatter(beside(hidden, seen_second))
        down_part = lax.psum_scatter(
            down_layer.reshape(n_ten, -1, 2 * slab), "tensor", scatter_dimension=0, tiled=False
        )
    else:
        down_sum = tn(hidden, seen_second)
        up_sum = tn(pre_grad, seen_middle)
    first_grad, mid_gain_part, mid_shift_part, out_bias_part = norm_back(
        middle_grad, unit_mid, inverse_mid, gain_mid
    )
    seen_first = both_rows(first_grad.astype(BF16))
    context_grad = nt(seen_first, w_out).astype(BF16)
    if small:
        up_block = beside(pre_grad, seen_middle)
        out_block = beside(context, seen_first)
        n_up = n_ten * units
        mid_layer = layer_scatter(
            lambda move: jnp.concatenate((up_block(move), out_block(move)), axis=0)
        )
        mid_layer = jnp.concatenate(
            (
                mid_layer[n_up:].reshape(n_ten, cols, 2 * slab),
                mid_layer[:n_up].reshape(n_ten, units, 2 * slab),
            ),
            axis=1,
        )
        mid_part = lax.psum_scatter(mid_layer, "tensor", scatter_dimension=0, tiled=False)
    else:
        out_sum = tn(context, seen_first)
    qkv_low, bias_sums = attend_back(joint, context_grad, context, lse, n_ten)
    input_grad = summed_rows(qkv_low, w_qkv, nn) + first_grad
    input_grad = swap(input_grad.astype(BF16)).astype(F32)

    def scattered(total):
        rows = total.shape[0] // n_ten
        blocks = (
            total.astype(BF16)
            .reshape(n_ten, rows, n_chip, 2 * slab)
            .transpose(2, 0, 1, 3)
            .reshape(n_chip * n_ten, rows, 2 * slab)
        )
        return lax.psum_scatter(blocks, CHIPS, scatter_dimension=0, tiled=False)

    wide = (
        mid_gain_part,
        mid_shift_part,
        out_bias_part,
        end_gain_part,
        end_shift_part,
        down_bias_part,
    )
    narrow = (bias_sums[:, 0], bias_sums[:, 1], up_bias_part)
    if small:
        tail = []
        for vector in wide:
            tail.append(vector.reshape(n_chip, 2, n_ten, -1).transpose(0, 2, 1, 3))
        for vector in narrow:
            tail.append(vector.reshape(n_chip, n_ten, 1, -1))
        tail = [t.reshape(n_chip * n_ten, -1) for t in tail]
        tail_sizes = [t.shape[1] for t in tail]
        used = sum(tail_sizes)
        lines = -(-used // (2 * slab))
        lines = -(-lines // 16) * 16
        extra = jnp.concatenate(
            tail + [jnp.zeros((n_chip * n_ten, lines * 2 * slab - used), F32)], axis=1
        )
        extra = extra.reshape(n_chip, n_ten * lines, 2 * slab).astype(BF16)
        qkv_block = beside(qkv_low, seen)

        def last_block(move):
            owner = lax.bitwise_xor(chip, move)
            mark = lax.dynamic_index_in_dim(extra, owner, 0, keepdims=False)
            return jnp.concatenate((qkv_block(move), mark), axis=0)

        last = layer_scatter(last_block)
        n_qkv = 3 * n_ten * cols
        last = jnp.concatenate(
            (
                last[:n_qkv].reshape(n_ten, 3 * cols, 2 * slab),
                last[n_qkv:].reshape(n_ten, lines, 2 * slab),
            ),
            axis=1,
        )
        qkv_part = lax.psum_scatter(last, "tensor", scatter_dimension=0, tiled=False)
        vector_line = qkv_part[3 * cols :].reshape(-1).astype(F32)
        qkv_part = qkv_part[: 3 * cols]
        parts = jnp.concatenate((qkv_part, mid_part, down_part), axis=0)
    else:
        qkv_sum = tn(qkv_low, seen)
        parts = jnp.concatenate([scattered(t) for t in (qkv_sum, out_sum, up_sum, down_sum)], axis=0)
    parts = parts.reshape(-1, 2, slab)
    keep = lax.dynamic_index_in_dim(parts, core, 1, keepdims=False)
    came = to_other(lax.dynamic_index_in_dim(parts, 1 - core, 1, keepdims=False))
    halves = jnp.stack(
        (jnp.where(core == 0, keep, came), jnp.where(core == 0, came, keep)), axis=0
    ).astype(F32)
    cut = [halves[:, bounds[i] : bounds[i + 1]] for i in range(4)]
    qkv_out = (
        cut[0].reshape(2, 3, cols, slab).transpose(3, 1, 0, 2).reshape(slab, 3, 2 * cols)
    )
    out_out = cut[1].reshape(2 * cols, slab)
    up_out = cut[2].reshape(2 * units, slab).T
    down_out = cut[3].reshape(2 * units, slab)

    if small:
        n_wide = sum(tail_sizes[:6])
        doubled = vector_line[:n_wide].reshape(6, 2, -1)
        own = lax.dynamic_index_in_dim(doubled, core, 1, keepdims=False)
        away = to_other(lax.dynamic_index_in_dim(doubled, 1 - core, 1, keepdims=False))
        own = own + away
        rest = vector_line[n_wide:]
        n_q, n_v, n_up = tail_sizes[6:]
        grads = [own[i] for i in range(6)] + [
            rest[:n_q],
            rest[n_q : n_q + n_v],
            rest[n_q + n_v : n_q + n_v + n_up],
        ]
    else:

        def placed(vector):
            blank = jnp.zeros((n_ten, 2, vector.size // n_ten), F32)
            return lax.dynamic_update_slice_in_dim(
                blank, vector.reshape(n_ten, 1, -1), core, 1
            ).reshape(-1)

        flat = list(wide) + [placed(v) for v in narrow]
        devices = n_chip * 2 * n_ten
        flat = [v.reshape(devices, -1) for v in flat]
        sums = lax.psum_scatter(
            jnp.concatenate(flat, axis=1), ALL, scatter_dimension=0, tiled=False
        )
        grads = []
        at = 0
        for v in flat:
            grads.append(sums[at : at + v.shape[1]])
            at += v.shape[1]
    g_mid_gain, g_mid_shift, g_out_bias, g_end_gain, g_end_shift, g_down_bias, g_q, g_v, g_up = (
        grads
    )
    return (
        encoded,
        input_grad,
        qkv_out,
        out_out,
        up_out,
        down_out,
        g_mid_gain,
        g_mid_shift,
        g_q,
        g_v,
        g_out_bias,
        g_end_gain,
        g_end_shift,
        g_up,
        g_down_bias,
    )


def solution(mesh):
    n_dp, n_ten = mesh.devices.shape
    inner = Mesh(mesh.devices.reshape(n_dp // 2, 2, n_ten), ALL)
    rows = P(ALL, None)
    vector = P(ALL)
    dp = ("chip", "core")
    weights = (P(dp, None, "tensor"), P("tensor", dp), P(dp, "tensor"), P("tensor", dp))
    return jax.shard_map(
        on_device,
        mesh=inner,
        in_specs=(rows, *weights, *(vector,) * 9, rows),
        out_specs=(rows, rows, *weights, *(vector,) * 9),
        check_vma=False,
    )
```

```python
import functools

import jax
import jax.numpy as jnp
from jax import lax
from jax.experimental import pallas as pl
from jax.experimental.pallas import tpu as pltpu
from jax.sharding import Mesh
from jax.sharding import PartitionSpec as P

HD = 64
LEN = 1024
PAIR = 2 * HD
QB = 256
VMEM = 56 * 1024 * 1024
ALL = ("chip", "core", "tensor")
CHIPS = ("chip", "tensor")
F32 = jnp.float32
BF16 = jnp.bfloat16
SCALE = HD ** (-0.5)
EPS = 1e-05


def nt(left, right):
    return lax.dot_general(left, right, (((1,), (1,)), ((), ())), preferred_element_type=F32)


def nn(left, right):
    return lax.dot_general(left, right, (((1,), (0,)), ((), ())), preferred_element_type=F32)


def tn(left, right):
    return lax.dot_general(left, right, (((0,), (0,)), ((), ())), preferred_element_type=F32)


def head_lane(rows, head):
    lane = lax.broadcasted_iota(jnp.int32, (rows, PAIR), 1)
    return (lane >= head * HD) & (lane < (head + 1) * HD)


def attend_kernel(q_ref, k_ref, v_ref, o_ref, lse_ref):
    rows = q_ref.shape[0]
    keys = k_ref[...]
    values_t = v_ref[...].astype(F32).T
    sub = lax.broadcasted_iota(jnp.int32, values_t.shape, 0)
    values_h = [
        jnp.where((sub >= h * HD) & (sub < (h + 1) * HD), values_t, 1.0).astype(BF16)
        for h in range(2)
    ]

    def block(step, carry):
        at = pl.ds(pl.multiple_of(step * QB, QB), QB)
        q = q_ref[at, :].astype(F32) * SCALE
        parts = []
        for h in range(2):
            qm = jnp.where(head_lane(QB, h), q, 0.0).astype(BF16)
            scores = nt(keys, qm)
            largest = jnp.max(scores, axis=0, keepdims=True)
            weights = jnp.exp(scores - largest).astype(BF16)
            out = nn(values_h[h], weights)
            total = out[(1 - h) * HD : (1 - h) * HD + 1, :]
            parts.append(out[h * HD : (h + 1) * HD, :] / total)
            lse_ref[0, h : h + 1, at] = largest + jnp.log(total)
        o_ref[at, :] = jnp.concatenate(parts, axis=0).T.astype(BF16)
        return carry

    lax.fori_loop(0, rows // QB, block, 0)


def without(count, kernel):
    def call(*refs):
        return kernel(*refs[count:])

    return call


def attend(joint, groups, first, last, so_far=()):
    rows = joint.shape[0]
    part = lambda c: pl.BlockSpec((rows, PAIR), lambda z: (0, 3 * (z + first) + c))
    kept = len(so_far)
    return pl.pallas_call(
        without(kept, attend_kernel),
        grid=(last - first,),
        in_specs=[pl.BlockSpec(memory_space=pl.ANY)] * kept + [part(0), part(1), part(2)],
        input_output_aliases={i: i for i in range(kept)},
        out_specs=[
            pl.BlockSpec((rows, PAIR), lambda z: (0, z + first)),
            pl.BlockSpec((1, 2, rows), lambda z: (z + first, 0, 0)),
        ],
        out_shape=[
            jax.ShapeDtypeStruct((rows, groups * PAIR), BF16),
            jax.ShapeDtypeStruct((groups, 2, rows), F32),
        ],
        compiler_params=pltpu.CompilerParams(vmem_limit_bytes=VMEM),
        cost_estimate=pl.CostEstimate(
            flops=(last - first) * 2 * rows * HD,
            bytes_accessed=(last - first) * rows,
            transcendentals=(last - first) * 2 * rows,
        ),
        name="attend",
    )(*so_far, joint, joint, joint)


def attend_back_kernel(q_ref, k_ref, v_ref, g_ref, o_ref, lse_ref, d_ref, sum_ref, dk_ref, dv_ref):
    rows = q_ref.shape[0]
    keys = k_ref[...]
    values = v_ref[...]
    keys_t = keys.astype(F32).T
    sub = lax.broadcasted_iota(jnp.int32, keys_t.shape, 0)
    keys_h = [
        jnp.where((sub >= h * HD) & (sub < (h + 1) * HD), keys_t, 0.0).astype(BF16)
        for h in range(2)
    ]
    dk_ref[...] = jnp.zeros_like(dk_ref)
    dv_ref[...] = jnp.zeros_like(dv_ref)

    def block(step, query_sum):
        at = pl.ds(pl.multiple_of(step * QB, QB), QB)
        q = q_ref[at, :].astype(F32) * SCALE
        g = g_ref[at, :].astype(F32)
        inner = (g * o_ref[at, :].astype(F32)).T
        dq = None
        for h in range(2):
            here = head_lane(QB, h)
            qm = jnp.where(here, q, 0.0).astype(BF16)
            gm = jnp.where(here, g, 0.0).astype(BF16)
            delta = jnp.sum(inner[h * HD : (h + 1) * HD, :], axis=0, keepdims=True)
            probs = jnp.exp(nt(keys, qm) - lse_ref[0, h : h + 1, at])
            score_grad = (probs * (nt(values, gm) - delta)).astype(BF16)
            dv_ref[...] += nn(probs.astype(BF16), gm)
            dk_ref[...] += nn(score_grad, qm)
            part = nn(keys_h[h], score_grad)
            dq = part if dq is None else dq + part
        dq = (dq.T * SCALE).astype(BF16)
        d_ref[at, 0:PAIR] = dq
        return query_sum + jnp.sum(dq.astype(F32), axis=0, keepdims=True)

    query_sum = lax.fori_loop(0, rows // QB, block, jnp.zeros((1, PAIR), F32))
    dv = dv_ref[...].astype(BF16)
    d_ref[:, PAIR : 2 * PAIR] = dk_ref[...].astype(BF16)
    d_ref[:, 2 * PAIR :] = dv
    sum_ref[0, 0:1, :] = query_sum
    sum_ref[0, 1:2, :] = jnp.sum(dv.astype(F32), axis=0, keepdims=True)


def attend_back(joint, context_grad, context, lse, groups, first, last, so_far=()):
    rows = joint.shape[0]
    part = lambda c: pl.BlockSpec((rows, PAIR), lambda z: (0, 3 * (z + first) + c))
    one = pl.BlockSpec((rows, PAIR), lambda z: (0, z + first))
    kept = len(so_far)
    return pl.pallas_call(
        without(kept, attend_back_kernel),
        grid=(last - first,),
        input_output_aliases={i: i for i in range(kept)},
        in_specs=[pl.BlockSpec(memory_space=pl.ANY)] * kept
        + [
            part(0),
            part(1),
            part(2),
            one,
            one,
            pl.BlockSpec((1, 2, rows), lambda z: (z + first, 0, 0)),
        ],
        out_specs=[
            pl.BlockSpec((rows, 3 * PAIR), lambda z: (0, z + first)),
            pl.BlockSpec((1, 2, PAIR), lambda z: (z + first, 0, 0)),
        ],
        out_shape=[
            jax.ShapeDtypeStruct((rows, 3 * groups * PAIR), BF16),
            jax.ShapeDtypeStruct((groups, 2, PAIR), F32),
        ],
        scratch_shapes=[pltpu.VMEM((rows, PAIR), F32), pltpu.VMEM((rows, PAIR), F32)],
        compiler_params=pltpu.CompilerParams(vmem_limit_bytes=VMEM),
        cost_estimate=pl.CostEstimate(
            flops=(last - first) * 2 * rows * HD,
            bytes_accessed=(last - first) * rows,
            transcendentals=(last - first) * 2 * rows,
        ),
        name="attend_back",
    )(*so_far, joint, joint, joint, context_grad, context, lse)


def normalized(values_in):
    average = jnp.mean(values_in, axis=-1, keepdims=True)
    centred = values_in - average
    inverse = lax.rsqrt(jnp.mean(centred * centred, axis=-1, keepdims=True) + EPS)
    return centred * inverse, inverse


def norm_back(grad, unit, inverse, gain):
    gain_part = jnp.sum(grad * unit, axis=0)
    shift_part = jnp.sum(grad, axis=0)
    u = grad * gain
    back = inverse * (
        u
        - jnp.mean(u, axis=-1, keepdims=True)
        - unit * jnp.mean(u * unit, axis=-1, keepdims=True)
    )
    return back, gain_part, shift_part, jnp.sum(back, axis=0)


def gelu_pair(x):
    phi = 0.5 * (1.0 + lax.erf(x * (0.5**0.5)))
    slope = phi + x * jnp.exp(-0.5 * x * x) * (0.5 / jnp.pi) ** 0.5
    return (x * phi).astype(BF16), slope.astype(BF16)


def to_other(value):
    return lax.ppermute(value, "core", [(0, 1), (1, 0)])


def both_rows(value):
    return jnp.concatenate((value, to_other(value)), axis=0)


def summed_rows(rows, weight, dot):
    half = rows.shape[0] // 2
    away = to_other(dot(rows[half:], weight).astype(BF16))
    return dot(rows[:half], weight) + away.astype(F32)


def assemble_kernel(n_far, chip_ref, own_ref, x_ref, y_ref, *refs):
    far_refs, out_refs = refs[:n_far], refs[n_far:]
    chip = chip_ref[0]
    wide = own_ref.shape[2]
    lower = pl.program_id(0) < pl.num_programs(0) // 2
    start = 0
    for out_ref in out_refs:
        rows = slice(start, start + out_ref.shape[1])
        start += out_ref.shape[1]

        def columns(move):
            at = pl.multiple_of(lax.bitwise_xor(chip, move) * wide, wide)
            return pl.ds(at, wide)

        out_ref[0, :, columns(0)] = own_ref[0, rows, :]
        out_ref[0, :, columns(1)] = x_ref[0, rows, :]
        out_ref[0, :, columns(2)] = y_ref[0, rows, :]
        far = far_refs[0][0, rows, :]
        if n_far == 2:
            far = jnp.where(lower, far, far_refs[1][0, rows, :])
        out_ref[0, :, columns(3)] = far


def assemble(chip, blocks, heights):
    own, low = blocks[0], blocks[3]
    members, rows, wide = own.shape
    half = low.shape[0]
    one = pl.BlockSpec((1, rows, wide), lambda z, c: (z, 0, 0))
    far = [pl.BlockSpec((1, rows, wide), lambda z, c: (jnp.minimum(z, half - 1), 0, 0))]
    if len(blocks) == 5:
        far.append(pl.BlockSpec((1, rows, wide), lambda z, c: (jnp.maximum(z - half, 0), 0, 0)))
    return pl.pallas_call(
        functools.partial(assemble_kernel, len(far)),
        grid_spec=pltpu.PrefetchScalarGridSpec(
            num_scalar_prefetch=1,
            grid=(members,),
            in_specs=[one, one, one, *far],
            out_specs=[pl.BlockSpec((1, h, 4 * wide), lambda z, c: (z, 0, 0)) for h in heights],
        ),
        out_shape=[jax.ShapeDtypeStruct((members, h, 4 * wide), BF16) for h in heights],
        compiler_params=pltpu.CompilerParams(vmem_limit_bytes=VMEM),
        cost_estimate=pl.CostEstimate(
            flops=0, bytes_accessed=members * rows, transcendentals=0
        ),
        name="assemble",
    )(chip.reshape(1), *blocks)


def to_chip(value, move):
    return lax.ppermute(value, "chip", [(i, i ^ move) for i in range(4)])


def after(value, *earlier):
    return lax.optimization_barrier((value, *earlier))[0]


def layer_near(part, ready=()):
    own = after(lax.all_gather(part, "tensor", axis=0, tiled=False), *ready)
    return own, to_chip(own, 1), to_chip(own, 2)


def layer_far(by_x, by_y):
    half = by_x.shape[0] // 2
    return to_chip(by_y[:half], 1), to_chip(by_x[half:], 2)


def scatter_far(block, ready=()):
    far = block(3)
    half = far.shape[0] // 2
    return to_chip(after(far[:half], *ready), 1), to_chip(after(far[half:], *ready), 2)


def scatter_near(block, low, high, ready=()):
    half = low.shape[0]
    near_x = block(1)
    near_y = block(2)
    add = lambda a, b: (a.astype(F32) + b.astype(F32)).astype(BF16)
    near_y = jnp.concatenate((add(near_y[:half], low), near_y[half:]), axis=0)
    near_x = jnp.concatenate((near_x[:half], add(near_x[half:], high)), axis=0)
    near_x = after(near_x, *ready)
    near_y = after(near_y, *ready)
    return block(0), to_chip(near_x, 1), to_chip(near_y, 2)


def three_sum(parts):
    return sum(p.astype(F32) for p in parts).astype(BF16)


def in_chip_order(chip, blocks):
    b0, b1, b2, b3 = blocks
    odd_x = (chip & 1) == 1
    odd_y = (chip & 2) == 2
    a0, a1 = jnp.where(odd_x, b1, b0), jnp.where(odd_x, b0, b1)
    a2, a3 = jnp.where(odd_x, b3, b2), jnp.where(odd_x, b2, b3)
    return jnp.stack(
        (
            jnp.where(odd_y, a2, a0),
            jnp.where(odd_y, a3, a1),
            jnp.where(odd_y, a0, a2),
            jnp.where(odd_y, a1, a3),
        )
    )


def on_device(
    tokens,
    qkv_weight,
    out_weight,
    up_weight,
    down_weight,
    mid_gain,
    mid_shift,
    query_bias,
    value_bias,
    out_bias,
    end_gain,
    end_shift,
    up_bias,
    down_bias,
    cotangent,
):
    core = lax.axis_index("core")
    chip = lax.axis_index("chip")
    n_chip = lax.axis_size("chip")
    n_ten = lax.axis_size("tensor")
    strip = tokens.shape[0]
    width = tokens.shape[1]
    slab = qkv_weight.shape[0]
    cols = qkv_weight.shape[2] // 2
    units = up_weight.shape[1] // 2
    assert 2 * strip == LEN and cols == PAIR

    pairs = []
    for z in range(n_ten):
        pairs.append((z, z) if z % 2 == 0 else (z, n_ten + z - 1))
        pairs.append((n_ten + z, z + 1) if z % 2 == 0 else (n_ten + z, n_ten + z))
    swap = lambda value: lax.ppermute(value, ("core", "tensor"), pairs)

    vectors = (
        mid_gain,
        mid_shift,
        query_bias,
        value_bias,
        out_bias,
        end_gain,
        end_shift,
        up_bias,
        down_bias,
    )
    stack = jnp.concatenate(
        (
            jnp.moveaxis(qkv_weight.reshape(slab, 3, 2, cols), 0, 3)
            .transpose(1, 0, 2, 3)
            .reshape(2, 3 * cols, slab),
            out_weight.reshape(2, cols, slab),
            up_weight.T.reshape(2, units, slab),
            down_weight.reshape(2, units, slab),
        ),
        axis=1,
    )
    keep = lax.dynamic_index_in_dim(stack, core, 0, keepdims=False)
    came = to_other(lax.dynamic_index_in_dim(stack, 1 - core, 0, keepdims=False))
    shard = jnp.concatenate(
        (jnp.where(core == 0, keep, came), jnp.where(core == 0, came, keep)), axis=1
    )
    bounds = (0, 3 * cols, 4 * cols, 4 * cols + units, 4 * cols + 2 * units)

    mine = swap(tokens)
    seen = both_rows(mine)
    sizes = [v.shape[0] for v in vectors]
    n_vec = sum(sizes)
    flat = jnp.concatenate(vectors)
    small = n_chip == 4 and n_ten == 4
    if small:
        coarse = lax.reduce_precision(flat, 8, 7)
        middle_bits = lax.reduce_precision(flat - coarse, 8, 7)
        thirds = jnp.concatenate((coarse, middle_bits, flat - coarse - middle_bits)).astype(BF16)
        came = to_other(thirds)
        both = jnp.concatenate(
            (jnp.where(core == 0, thirds, came), jnp.where(core == 0, came, thirds))
        )
        lines = -(-both.size // (16 * 2 * slab)) * 16
        both = jnp.concatenate((both, jnp.zeros((lines * 2 * slab - both.size,), BF16)))
        first = jnp.concatenate((shard[: bounds[1]], both.reshape(lines, 2 * slab)), axis=0)
        third = shard[bounds[3] :][None]
        third = (third, *(to_chip(third, move) for move in (1, 2, 3)))
        blocks = layer_near(first, (mine, *third[1:]))
        blocks += layer_far(*blocks[1:])
        (w_qkv,) = assemble(chip, blocks, (3 * cols,))
        tails = [b[:, 3 * cols :] for b in blocks]
        tails = tails[:3] + [jnp.concatenate(tails[3:], axis=0)]
        packed = in_chip_order(chip, tails).reshape(n_chip, n_ten, -1)[:, :, : 6 * n_vec]
        packed = packed.reshape(n_chip, n_ten, 2, 3, n_vec).astype(F32)
        packed = packed[:, :, :, 0] + packed[:, :, :, 1] + packed[:, :, :, 2]
        packed = packed.transpose(0, 2, 1, 3).reshape(-1, n_vec)
        second = after(shard[bounds[1] : bounds[3]], blocks[0])
        mid_blocks = layer_near(second)
        (third,) = assemble(chip, third, (units,))
        w_down = lax.all_gather(after(third[0], mid_blocks[0]), "tensor", axis=0, tiled=True)
        cot = swap(after(cotangent, w_down))
        w_qkv = w_qkv.reshape(-1, width)
    else:

        def gathered(index):
            part = shard[bounds[index] : bounds[index + 1]]
            rows = part.shape[0]
            full = lax.all_gather(part, CHIPS, axis=0, tiled=False)
            return (
                full.reshape(n_chip, n_ten, rows, 2 * slab)
                .transpose(1, 2, 0, 3)
                .reshape(n_ten * rows, width)
            )

        w_qkv, w_out, w_up, w_down = (gathered(i) for i in range(4))
        packed = lax.all_gather(flat, ALL, axis=0, tiled=False)
    starts = [sum(sizes[:i]) for i in range(len(sizes))]
    whole = [packed[:, s : s + n].reshape(-1) for s, n in zip(starts, sizes)]
    gain_mid, shift_mid, bias_q, bias_v, bias_out, gain_end, shift_end, bias_up, bias_down = whole

    def own_half(vector):
        return lax.dynamic_index_in_dim(vector.reshape(n_ten, 2, -1), core, 1, keepdims=False)

    bias_q, bias_v, bias_up = own_half(bias_q), own_half(bias_v), own_half(bias_up)
    bias_qkv = jnp.stack((bias_q, jnp.zeros_like(bias_q), bias_v), axis=1).reshape(-1)
    bias_up = bias_up.reshape(-1)

    joint = (nt(seen, w_qkv) + bias_qkv).astype(BF16)
    if not small:
        cot = swap(cotangent)
    half = n_ten // 2
    context, lse = attend(joint, n_ten, 0, half)
    if small:
        far = layer_far(*(after(block, context) for block in mid_blocks[1:]))
        context = after(context, *mid_blocks[1:])
    context, lse = attend(joint, n_ten, half, n_ten, (context, lse))
    if small:
        w_out, w_up = assemble(chip, (after(mid_blocks[0], context), *mid_blocks[1:], *far), (cols, units))
        w_out, w_up = w_out.reshape(-1, width), w_up.reshape(-1, width)
    branch = summed_rows(context, w_out, nn)
    unit_mid, inverse_mid = normalized(mine.astype(F32) + branch + bias_out)
    middle = unit_mid * gain_mid + shift_mid
    seen_middle = both_rows(middle.astype(BF16))
    hidden, slope = gelu_pair(nt(seen_middle, w_up) + bias_up)
    branch_two = summed_rows(hidden, w_down, nn)
    unit_end, inverse_end = normalized(middle + branch_two + bias_down)
    encoded = (unit_end * gain_end + shift_end).astype(BF16)

    second_grad, end_gain_part, end_shift_part, down_bias_part = norm_back(
        cot.astype(F32), unit_end, inverse_end, gain_end
    )
    seen_second = both_rows(second_grad.astype(BF16))
    pre_grad = (nt(seen_second, w_down) * slope.astype(F32)).astype(BF16)
    up_bias_part = jnp.sum(pre_grad.astype(F32), axis=0)
    middle_grad = summed_rows(pre_grad, w_up, nn) + second_grad

    def member_sum(total):
        total = total.reshape(n_ten, -1, 2 * slab)
        return lax.psum_scatter(total, "tensor", scatter_dimension=0, tiled=False)

    def beside(rows, columns):
        def block(move):
            at = lax.bitwise_xor(chip, move) * (2 * slab)
            return tn(rows, lax.dynamic_slice_in_dim(columns, at, 2 * slab, axis=1)).astype(BF16)

        return block

    if small:
        down_sum = tn(hidden, seen_second).astype(BF16)
        down_rows = lax.psum_scatter(
            down_sum.reshape(n_ten, units, width), "tensor", scatter_dimension=0, tiled=False
        )
        up_block = beside(pre_grad, after(seen_middle, down_sum))
        up_far = scatter_far(up_block)
    else:
        down_sum = tn(hidden, seen_second)
        up_sum = tn(pre_grad, seen_middle)
    first_grad, mid_gain_part, mid_shift_part, out_bias_part = norm_back(
        middle_grad, unit_mid, inverse_mid, gain_mid
    )
    seen_first = both_rows(first_grad.astype(BF16))
    if small:
        up_far = [after(part, first_grad) for part in up_far]
        up_layer = scatter_near(up_block, *up_far)
    context_grad = nt(seen_first, w_out).astype(BF16)
    if not small:
        out_sum = tn(context, seen_first)
    given = (joint, context_grad, context, lse, n_ten)
    half_back = attend_back(*given, 0, half)
    if small:
        up_total = three_sum((after(up_layer[0], half_back[0]), *up_layer[1:]))
        half_back = (after(half_back[0], up_total), half_back[1])
    qkv_low, bias_sums = attend_back(*given, half, n_ten, half_back)
    if small:
        up_part = member_sum(up_total)
        encoded = after(encoded, up_part)
    encoded = swap(encoded)
    input_grad = summed_rows(qkv_low, w_qkv, nn) + first_grad
    input_grad = swap(input_grad.astype(BF16)).astype(F32)

    def core_halves(part):
        keep = lax.dynamic_slice_in_dim(part, core * slab, slab, axis=1)
        came = to_other(lax.dynamic_slice_in_dim(part, (1 - core) * slab, slab, axis=1))
        return jnp.stack(
            (jnp.where(core == 0, keep, came), jnp.where(core == 0, came, keep)), axis=0
        ).astype(F32)

    def scattered(total):
        rows = total.shape[0] // n_ten
        blocks = (
            total.astype(BF16)
            .reshape(n_ten, rows, n_chip, 2 * slab)
            .transpose(2, 0, 1, 3)
            .reshape(n_chip * n_ten, rows, 2 * slab)
        )
        return lax.psum_scatter(blocks, CHIPS, scatter_dimension=0, tiled=False)

    wide = (
        mid_gain_part,
        mid_shift_part,
        out_bias_part,
        end_gain_part,
        end_shift_part,
        down_bias_part,
    )
    narrow = (bias_sums[:, 0], bias_sums[:, 1], up_bias_part)
    if small:
        tail = []
        for vector in wide:
            tail.append(vector.reshape(n_chip, 2, n_ten, -1).transpose(0, 2, 1, 3))
        for vector in narrow:
            tail.append(vector.reshape(n_chip, n_ten, 1, -1))
        tail = [t.reshape(n_chip * n_ten, -1) for t in tail]
        tail_sizes = [t.shape[1] for t in tail]
        used = sum(tail_sizes)
        lines = -(-used // (2 * slab))
        lines = -(-lines // 16) * 16
        extra = jnp.concatenate(
            tail + [jnp.zeros((n_chip * n_ten, lines * 2 * slab - used), F32)], axis=1
        )
        extra = extra.reshape(n_chip, n_ten * lines, 2 * slab).astype(BF16)
        out_block = beside(context, seen_first)

        def last_block(move):
            owner = lax.bitwise_xor(chip, move)
            mark = lax.dynamic_index_in_dim(extra, owner, 0, keepdims=False)
            return jnp.concatenate(
                (beside(qkv_low, seen)(move), out_block(move), mark), axis=0
            )

        last = scatter_near(last_block, *scatter_far(last_block, (down_rows,)), (up_part,))
        last = three_sum((after(last[0], input_grad, encoded), *last[1:]))
        n_qkv = 3 * n_ten * cols
        n_out = n_ten * cols
        last = jnp.concatenate(
            (
                last[:n_qkv].reshape(n_ten, 3 * cols, 2 * slab),
                last[n_qkv : n_qkv + n_out].reshape(n_ten, cols, 2 * slab),
                last[n_qkv + n_out :].reshape(n_ten, lines, 2 * slab),
            ),
            axis=1,
        )
        down_cut = lambda move: lax.dynamic_slice_in_dim(
            down_rows, lax.bitwise_xor(chip, move) * (2 * slab), 2 * slab, axis=1
        )
        down_part = three_sum([down_cut(0)] + [to_chip(down_cut(move), move) for move in (1, 2, 3)])
        last_part = member_sum(last)
        vector_line = last_part[4 * cols :].reshape(-1).astype(F32)
        last_halves = core_halves(last_part[: 4 * cols])
        cut = [
            last_halves[:, : 3 * cols],
            last_halves[:, 3 * cols :],
            core_halves(up_part),
            core_halves(down_part),
        ]
    else:
        qkv_sum = tn(qkv_low, seen)
        parts = jnp.concatenate([scattered(t) for t in (qkv_sum, out_sum, up_sum, down_sum)], axis=0)
        halves = core_halves(parts)
        cut = [halves[:, bounds[i] : bounds[i + 1]] for i in range(4)]
    qkv_out = (
        cut[0].reshape(2, 3, cols, slab).transpose(3, 1, 0, 2).reshape(slab, 3, 2 * cols)
    )
    out_out = cut[1].reshape(2 * cols, slab)
    up_out = cut[2].reshape(2 * units, slab).T
    down_out = cut[3].reshape(2 * units, slab)

    if small:
        n_wide = sum(tail_sizes[:6])
        doubled = vector_line[:n_wide].reshape(6, 2, -1)
        own = lax.dynamic_index_in_dim(doubled, core, 1, keepdims=False)
        away = to_other(lax.dynamic_index_in_dim(doubled, 1 - core, 1, keepdims=False))
        own = own + away
        rest = vector_line[n_wide:]
        n_q, n_v, n_up = tail_sizes[6:]
        grads = [own[i] for i in range(6)] + [
            rest[:n_q],
            rest[n_q : n_q + n_v],
            rest[n_q + n_v : n_q + n_v + n_up],
        ]
    else:

        def placed(vector):
            blank = jnp.zeros((n_ten, 2, vector.size // n_ten), F32)
            return lax.dynamic_update_slice_in_dim(
                blank, vector.reshape(n_ten, 1, -1), core, 1
            ).reshape(-1)

        flat = list(wide) + [placed(v) for v in narrow]
        devices = n_chip * 2 * n_ten
        flat = [v.reshape(devices, -1) for v in flat]
        sums = lax.psum_scatter(
            jnp.concatenate(flat, axis=1), ALL, scatter_dimension=0, tiled=False
        )
        grads = []
        at = 0
        for v in flat:
            grads.append(sums[at : at + v.shape[1]])
            at += v.shape[1]
    g_mid_gain, g_mid_shift, g_out_bias, g_end_gain, g_end_shift, g_down_bias, g_q, g_v, g_up = (
        grads
    )
    return (
        encoded,
        input_grad,
        qkv_out,
        out_out,
        up_out,
        down_out,
        g_mid_gain,
        g_mid_shift,
        g_q,
        g_v,
        g_out_bias,
        g_end_gain,
        g_end_shift,
        g_up,
        g_down_bias,
    )


def solution(mesh):
    n_dp, n_ten = mesh.devices.shape
    inner = Mesh(mesh.devices.reshape(n_dp // 2, 2, n_ten), ALL)
    rows = P(ALL, None)
    vector = P(ALL)
    dp = ("chip", "core")
    weights = (P(dp, None, "tensor"), P("tensor", dp), P(dp, "tensor"), P("tensor", dp))
    return jax.shard_map(
        on_device,
        mesh=inner,
        in_specs=(rows, *weights, *(vector,) * 9, rows),
        out_specs=(rows, rows, *weights, *(vector,) * 9),
        check_vma=False,
    )
```

```python
import functools

import jax
import jax.numpy as jnp
from jax import lax
from jax.experimental import pallas as pl
from jax.experimental.pallas import tpu as pltpu
from jax.sharding import Mesh
from jax.sharding import PartitionSpec as P

HD = 64
LEN = 1024
PAIR = 2 * HD
QB = 1024
VMEM = 56 * 1024 * 1024
ALL = ("chip", "core", "tensor")
CHIPS = ("chip", "tensor")
F32 = jnp.float32
BF16 = jnp.bfloat16
SCALE = HD ** (-0.5)
EPS = 1e-05


def nt(left, right):
    return lax.dot_general(left, right, (((1,), (1,)), ((), ())), preferred_element_type=F32)


def nn(left, right):
    return lax.dot_general(left, right, (((1,), (0,)), ((), ())), preferred_element_type=F32)


def tn(left, right):
    return lax.dot_general(left, right, (((0,), (0,)), ((), ())), preferred_element_type=F32)


def head_lane(rows, head):
    lane = lax.broadcasted_iota(jnp.int32, (rows, PAIR), 1)
    return (lane >= head * HD) & (lane < (head + 1) * HD)


def attend_kernel(q_ref, k_ref, v_ref, o_ref, lse_ref):
    rows = q_ref.shape[0]
    keys = k_ref[...]
    values_t = v_ref[...].astype(F32).T
    sub = lax.broadcasted_iota(jnp.int32, values_t.shape, 0)
    values_h = [
        jnp.where((sub >= h * HD) & (sub < (h + 1) * HD), values_t, 1.0).astype(BF16)
        for h in range(2)
    ]

    def block(step, carry):
        at = pl.ds(pl.multiple_of(step * QB, QB), QB)
        q = q_ref[at, :].astype(F32) * SCALE
        parts = []
        for h in range(2):
            qm = jnp.where(head_lane(QB, h), q, 0.0).astype(BF16)
            scores = nt(keys, qm)
            largest = jnp.max(scores, axis=0, keepdims=True)
            weights = jnp.exp(scores - largest).astype(BF16)
            out = nn(values_h[h], weights)
            total = out[(1 - h) * HD : (1 - h) * HD + 1, :]
            parts.append(out[h * HD : (h + 1) * HD, :] / total)
            lse_ref[0, h : h + 1, at] = largest + jnp.log(total)
        o_ref[at, :] = jnp.concatenate(parts, axis=0).T.astype(BF16)
        return carry

    lax.fori_loop(0, rows // QB, block, 0)


def without(count, kernel):
    def call(*refs):
        return kernel(*refs[count:])

    return call


def attend(joint, groups, first, last, so_far=()):
    rows = joint.shape[0]
    part = lambda c: pl.BlockSpec((rows, PAIR), lambda z: (0, 3 * (z + first) + c))
    kept = len(so_far)
    return pl.pallas_call(
        without(kept, attend_kernel),
        grid=(last - first,),
        in_specs=[pl.BlockSpec(memory_space=pl.ANY)] * kept + [part(0), part(1), part(2)],
        input_output_aliases={i: i for i in range(kept)},
        out_specs=[
            pl.BlockSpec((rows, PAIR), lambda z: (0, z + first)),
            pl.BlockSpec((1, 2, rows), lambda z: (z + first, 0, 0)),
        ],
        out_shape=[
            jax.ShapeDtypeStruct((rows, groups * PAIR), BF16),
            jax.ShapeDtypeStruct((groups, 2, rows), F32),
        ],
        compiler_params=pltpu.CompilerParams(vmem_limit_bytes=VMEM),
        cost_estimate=pl.CostEstimate(
            flops=(last - first) * 2 * rows * HD,
            bytes_accessed=(last - first) * rows,
            transcendentals=(last - first) * 2 * rows,
        ),
        name="attend",
    )(*so_far, joint, joint, joint)


def attend_back_kernel(q_ref, k_ref, v_ref, g_ref, o_ref, lse_ref, d_ref, sum_ref, dk_ref, dv_ref):
    rows = q_ref.shape[0]
    keys = k_ref[...]
    values = v_ref[...]
    keys_t = keys.astype(F32).T
    sub = lax.broadcasted_iota(jnp.int32, keys_t.shape, 0)
    keys_h = [
        jnp.where((sub >= h * HD) & (sub < (h + 1) * HD), keys_t, 0.0).astype(BF16)
        for h in range(2)
    ]
    dk_ref[...] = jnp.zeros_like(dk_ref)
    dv_ref[...] = jnp.zeros_like(dv_ref)

    def block(step, query_sum):
        at = pl.ds(pl.multiple_of(step * QB, QB), QB)
        q = q_ref[at, :].astype(F32) * SCALE
        g = g_ref[at, :].astype(F32)
        inner = (g * o_ref[at, :].astype(F32)).T
        dq = None
        for h in range(2):
            here = head_lane(QB, h)
            qm = jnp.where(here, q, 0.0).astype(BF16)
            gm = jnp.where(here, g, 0.0).astype(BF16)
            delta = jnp.sum(inner[h * HD : (h + 1) * HD, :], axis=0, keepdims=True)
            probs = jnp.exp(nt(keys, qm) - lse_ref[0, h : h + 1, at])
            score_grad = (probs * (nt(values, gm) - delta)).astype(BF16)
            dv_ref[...] += nn(probs.astype(BF16), gm)
            dk_ref[...] += nn(score_grad, qm)
            part = nn(keys_h[h], score_grad)
            dq = part if dq is None else dq + part
        dq = (dq.T * SCALE).astype(BF16)
        d_ref[at, 0:PAIR] = dq
        return query_sum + jnp.sum(dq.astype(F32), axis=0, keepdims=True)

    query_sum = lax.fori_loop(0, rows // QB, block, jnp.zeros((1, PAIR), F32))
    dv = dv_ref[...].astype(BF16)
    d_ref[:, PAIR : 2 * PAIR] = dk_ref[...].astype(BF16)
    d_ref[:, 2 * PAIR :] = dv
    sum_ref[0, 0:1, :] = query_sum
    sum_ref[0, 1:2, :] = jnp.sum(dv.astype(F32), axis=0, keepdims=True)


def attend_back(joint, context_grad, context, lse, groups, first, last, so_far=()):
    rows = joint.shape[0]
    part = lambda c: pl.BlockSpec((rows, PAIR), lambda z: (0, 3 * (z + first) + c))
    one = pl.BlockSpec((rows, PAIR), lambda z: (0, z + first))
    kept = len(so_far)
    return pl.pallas_call(
        without(kept, attend_back_kernel),
        grid=(last - first,),
        input_output_aliases={i: i for i in range(kept)},
        in_specs=[pl.BlockSpec(memory_space=pl.ANY)] * kept
        + [
            part(0),
            part(1),
            part(2),
            one,
            one,
            pl.BlockSpec((1, 2, rows), lambda z: (z + first, 0, 0)),
        ],
        out_specs=[
            pl.BlockSpec((rows, 3 * PAIR), lambda z: (0, z + first)),
            pl.BlockSpec((1, 2, PAIR), lambda z: (z + first, 0, 0)),
        ],
        out_shape=[
            jax.ShapeDtypeStruct((rows, 3 * groups * PAIR), BF16),
            jax.ShapeDtypeStruct((groups, 2, PAIR), F32),
        ],
        scratch_shapes=[pltpu.VMEM((rows, PAIR), F32), pltpu.VMEM((rows, PAIR), F32)],
        compiler_params=pltpu.CompilerParams(vmem_limit_bytes=VMEM),
        cost_estimate=pl.CostEstimate(
            flops=(last - first) * 2 * rows * HD,
            bytes_accessed=(last - first) * rows,
            transcendentals=(last - first) * 2 * rows,
        ),
        name="attend_back",
    )(*so_far, joint, joint, joint, context_grad, context, lse)


def normalized(values_in):
    average = jnp.mean(values_in, axis=-1, keepdims=True)
    centred = values_in - average
    inverse = lax.rsqrt(jnp.mean(centred * centred, axis=-1, keepdims=True) + EPS)
    return centred * inverse, inverse


def norm_back(grad, unit, inverse, gain):
    gain_part = jnp.sum(grad * unit, axis=0)
    shift_part = jnp.sum(grad, axis=0)
    u = grad * gain
    back = inverse * (
        u
        - jnp.mean(u, axis=-1, keepdims=True)
        - unit * jnp.mean(u * unit, axis=-1, keepdims=True)
    )
    return back, gain_part, shift_part, jnp.sum(back, axis=0)


def gelu_pair(x):
    phi = 0.5 * (1.0 + lax.erf(x * (0.5**0.5)))
    slope = phi + x * jnp.exp(-0.5 * x * x) * (0.5 / jnp.pi) ** 0.5
    return (x * phi).astype(BF16), slope.astype(BF16)


def to_other(value):
    return lax.ppermute(value, "core", [(0, 1), (1, 0)])


def both_rows(value):
    return jnp.concatenate((value, to_other(value)), axis=0)


def summed_rows(rows, weight, dot, ready=()):
    half = rows.shape[0] // 2
    away = to_other(after(dot(rows[half:], weight).astype(BF16), *ready))
    return dot(rows[:half], weight) + away.astype(F32)


def assemble_kernel(n_far, chip_ref, own_ref, x_ref, y_ref, *refs):
    far_refs, out_refs = refs[:n_far], refs[n_far:]
    chip = chip_ref[0]
    wide = own_ref.shape[2]
    lower = pl.program_id(0) < pl.num_programs(0) // 2
    start = 0
    for out_ref in out_refs:
        rows = slice(start, start + out_ref.shape[1])
        start += out_ref.shape[1]

        def columns(move):
            at = pl.multiple_of(lax.bitwise_xor(chip, move) * wide, wide)
            return pl.ds(at, wide)

        out_ref[0, :, columns(0)] = own_ref[0, rows, :]
        out_ref[0, :, columns(1)] = x_ref[0, rows, :]
        out_ref[0, :, columns(2)] = y_ref[0, rows, :]
        far = far_refs[0][0, rows, :]
        if n_far == 2:
            far = jnp.where(lower, far, far_refs[1][0, rows, :])
        out_ref[0, :, columns(3)] = far


def assemble(chip, blocks, heights):
    own, low = blocks[0], blocks[3]
    members, rows, wide = own.shape
    half = low.shape[0]
    one = pl.BlockSpec((1, rows, wide), lambda z, c: (z, 0, 0))
    far = [pl.BlockSpec((1, rows, wide), lambda z, c: (jnp.minimum(z, half - 1), 0, 0))]
    if len(blocks) == 5:
        far.append(pl.BlockSpec((1, rows, wide), lambda z, c: (jnp.maximum(z - half, 0), 0, 0)))
    return pl.pallas_call(
        functools.partial(assemble_kernel, len(far)),
        grid_spec=pltpu.PrefetchScalarGridSpec(
            num_scalar_prefetch=1,
            grid=(members,),
            in_specs=[one, one, one, *far],
            out_specs=[pl.BlockSpec((1, h, 4 * wide), lambda z, c: (z, 0, 0)) for h in heights],
        ),
        out_shape=[jax.ShapeDtypeStruct((members, h, 4 * wide), BF16) for h in heights],
        compiler_params=pltpu.CompilerParams(vmem_limit_bytes=VMEM),
        cost_estimate=pl.CostEstimate(
            flops=0, bytes_accessed=members * rows, transcendentals=0
        ),
        name="assemble",
    )(chip.reshape(1), *blocks)


def to_chip(value, move):
    return lax.ppermute(value, "chip", [(i, i ^ move) for i in range(4)])


def after(value, *earlier):
    return lax.optimization_barrier((value, *earlier))[0]


def layer_near(part, ready=()):
    own = after(lax.all_gather(part, "tensor", axis=0, tiled=False), *ready)
    return own, to_chip(own, 1), to_chip(own, 2)


def layer_far(by_x, by_y):
    half = by_x.shape[0] // 2
    return to_chip(by_y[:half], 1), to_chip(by_x[half:], 2)


def scatter_far(block, ready=()):
    far = block(3)
    half = far.shape[0] // 2
    return to_chip(after(far[:half], *ready), 1), to_chip(after(far[half:], *ready), 2)


def scatter_near(block, low, high, ready=()):
    half = low.shape[0]
    near_x = block(1)
    near_y = block(2)
    add = lambda a, b: (a.astype(F32) + b.astype(F32)).astype(BF16)
    near_y = jnp.concatenate((add(near_y[:half], low), near_y[half:]), axis=0)
    near_x = jnp.concatenate((near_x[:half], add(near_x[half:], high)), axis=0)
    near_x = after(near_x, *ready)
    near_y = after(near_y, *ready)
    return block(0), to_chip(near_x, 1), to_chip(near_y, 2)


def three_sum(parts):
    return sum(p.astype(F32) for p in parts).astype(BF16)


def in_chip_order(chip, blocks):
    b0, b1, b2, b3 = blocks
    odd_x = (chip & 1) == 1
    odd_y = (chip & 2) == 2
    a0, a1 = jnp.where(odd_x, b1, b0), jnp.where(odd_x, b0, b1)
    a2, a3 = jnp.where(odd_x, b3, b2), jnp.where(odd_x, b2, b3)
    return jnp.stack(
        (
            jnp.where(odd_y, a2, a0),
            jnp.where(odd_y, a3, a1),
            jnp.where(odd_y, a0, a2),
            jnp.where(odd_y, a1, a3),
        )
    )


def on_device(
    tokens,
    qkv_weight,
    out_weight,
    up_weight,
    down_weight,
    mid_gain,
    mid_shift,
    query_bias,
    value_bias,
    out_bias,
    end_gain,
    end_shift,
    up_bias,
    down_bias,
    cotangent,
):
    core = lax.axis_index("core")
    chip = lax.axis_index("chip")
    n_chip = lax.axis_size("chip")
    n_ten = lax.axis_size("tensor")
    strip = tokens.shape[0]
    width = tokens.shape[1]
    slab = qkv_weight.shape[0]
    cols = qkv_weight.shape[2] // 2
    units = up_weight.shape[1] // 2
    assert 2 * strip == LEN and cols == PAIR

    pairs = []
    for z in range(n_ten):
        pairs.append((z, z) if z % 2 == 0 else (z, n_ten + z - 1))
        pairs.append((n_ten + z, z + 1) if z % 2 == 0 else (n_ten + z, n_ten + z))
    swap = lambda value: lax.ppermute(value, ("core", "tensor"), pairs)

    vectors = (
        mid_gain,
        mid_shift,
        query_bias,
        value_bias,
        out_bias,
        end_gain,
        end_shift,
        up_bias,
        down_bias,
    )
    stack = jnp.concatenate(
        (
            jnp.moveaxis(qkv_weight.reshape(slab, 3, 2, cols), 0, 3)
            .transpose(1, 0, 2, 3)
            .reshape(2, 3 * cols, slab),
            out_weight.reshape(2, cols, slab),
            up_weight.T.reshape(2, units, slab),
            down_weight.reshape(2, units, slab),
        ),
        axis=1,
    )
    keep = lax.dynamic_index_in_dim(stack, core, 0, keepdims=False)
    came = to_other(lax.dynamic_index_in_dim(stack, 1 - core, 0, keepdims=False))
    shard = jnp.concatenate(
        (jnp.where(core == 0, keep, came), jnp.where(core == 0, came, keep)), axis=1
    )
    bounds = (0, 3 * cols, 4 * cols, 4 * cols + units, 4 * cols + 2 * units)

    mine = swap(tokens)
    seen = both_rows(mine)
    sizes = [v.shape[0] for v in vectors]
    n_vec = sum(sizes)
    flat = jnp.concatenate(vectors)
    small = n_chip == 4 and n_ten == 4
    if small:
        coarse = lax.reduce_precision(flat, 8, 7)
        middle_bits = lax.reduce_precision(flat - coarse, 8, 7)
        thirds = jnp.concatenate((coarse, middle_bits, flat - coarse - middle_bits)).astype(BF16)
        came = to_other(thirds)
        both = jnp.concatenate(
            (jnp.where(core == 0, thirds, came), jnp.where(core == 0, came, thirds))
        )
        lines = -(-both.size // (16 * 2 * slab)) * 16
        both = jnp.concatenate((both, jnp.zeros((lines * 2 * slab - both.size,), BF16)))
        first = jnp.concatenate((shard[: bounds[1]], both.reshape(lines, 2 * slab)), axis=0)
        third = shard[bounds[3] :][None]
        third = (third, *(to_chip(third, move) for move in (1, 2, 3)))
        blocks = layer_near(first, (mine, *third[1:]))
        blocks += layer_far(*blocks[1:])
        (w_qkv,) = assemble(chip, blocks, (3 * cols,))
        tails = [b[:, 3 * cols :] for b in blocks]
        tails = tails[:3] + [jnp.concatenate(tails[3:], axis=0)]
        packed = in_chip_order(chip, tails).reshape(n_chip, n_ten, -1)[:, :, : 6 * n_vec]
        packed = packed.reshape(n_chip, n_ten, 2, 3, n_vec).astype(F32)
        packed = packed[:, :, :, 0] + packed[:, :, :, 1] + packed[:, :, :, 2]
        packed = packed.transpose(0, 2, 1, 3).reshape(-1, n_vec)
        second = after(shard[bounds[1] : bounds[3]], blocks[0])
        mid_blocks = layer_near(second)
        (third,) = assemble(chip, third, (units,))
        w_down = lax.all_gather(after(third[0], blocks[1]), "tensor", axis=0, tiled=True)
        w_qkv = w_qkv.reshape(-1, width)
    else:

        def gathered(index):
            part = shard[bounds[index] : bounds[index + 1]]
            rows = part.shape[0]
            full = lax.all_gather(part, CHIPS, axis=0, tiled=False)
            return (
                full.reshape(n_chip, n_ten, rows, 2 * slab)
                .transpose(1, 2, 0, 3)
                .reshape(n_ten * rows, width)
            )

        w_qkv, w_out, w_up, w_down = (gathered(i) for i in range(4))
        packed = lax.all_gather(flat, ALL, axis=0, tiled=False)
    starts = [sum(sizes[:i]) for i in range(len(sizes))]
    whole = [packed[:, s : s + n].reshape(-1) for s, n in zip(starts, sizes)]
    gain_mid, shift_mid, bias_q, bias_v, bias_out, gain_end, shift_end, bias_up, bias_down = whole

    def own_half(vector):
        return lax.dynamic_index_in_dim(vector.reshape(n_ten, 2, -1), core, 1, keepdims=False)

    bias_q, bias_v, bias_up = own_half(bias_q), own_half(bias_v), own_half(bias_up)
    bias_qkv = jnp.stack((bias_q, jnp.zeros_like(bias_q), bias_v), axis=1).reshape(-1)
    bias_up = bias_up.reshape(-1)

    joint = (nt(seen, w_qkv) + bias_qkv).astype(BF16)
    half = n_ten // 2
    context, lse = attend(joint, n_ten, 0, half)
    if small:
        far = layer_far(*(after(block, context) for block in mid_blocks[1:]))
        context = after(context, *mid_blocks[1:])
    context, lse = attend(joint, n_ten, half, n_ten, (context, lse))
    if small:
        w_out, w_up = assemble(chip, (after(mid_blocks[0], context), *mid_blocks[1:], *far), (cols, units))
        w_out, w_up = w_out.reshape(-1, width), w_up.reshape(-1, width)
    branch = summed_rows(context, w_out, nn)
    unit_mid, inverse_mid = normalized(mine.astype(F32) + branch + bias_out)
    middle = unit_mid * gain_mid + shift_mid
    seen_middle = both_rows(middle.astype(BF16))
    hidden, slope = gelu_pair(nt(seen_middle, w_up) + bias_up)
    cot = swap(after(cotangent, w_down, hidden))
    branch_two = summed_rows(hidden, w_down, nn)
    unit_end, inverse_end = normalized(middle + branch_two + bias_down)
    encoded = (unit_end * gain_end + shift_end).astype(BF16)

    second_grad, end_gain_part, end_shift_part, down_bias_part = norm_back(
        cot.astype(F32), unit_end, inverse_end, gain_end
    )
    seen_second = both_rows(second_grad.astype(BF16))
    pre_grad = (nt(seen_second, w_down) * slope.astype(F32)).astype(BF16)
    up_bias_part = jnp.sum(pre_grad.astype(F32), axis=0)
    middle_grad = summed_rows(pre_grad, w_up, nn) + second_grad

    def member_sum(total):
        total = total.reshape(n_ten, -1, 2 * slab)
        return lax.psum_scatter(total, "tensor", scatter_dimension=0, tiled=False)

    def beside(rows, columns):
        def block(move):
            at = lax.bitwise_xor(chip, move) * (2 * slab)
            return tn(rows, lax.dynamic_slice_in_dim(columns, at, 2 * slab, axis=1)).astype(BF16)

        return block

    if small:
        down_sum = tn(hidden, seen_second).astype(BF16)
        down_rows = lax.psum_scatter(
            down_sum.reshape(n_ten, units, width), "tensor", scatter_dimension=0, tiled=False
        )
        up_block = beside(pre_grad, after(seen_middle, down_sum))
        up_far = scatter_far(up_block)
    else:
        down_sum = tn(hidden, seen_second)
        up_sum = tn(pre_grad, seen_middle)
    first_grad, mid_gain_part, mid_shift_part, out_bias_part = norm_back(
        middle_grad, unit_mid, inverse_mid, gain_mid
    )
    seen_first = both_rows(first_grad.astype(BF16))
    context_grad = nt(seen_first, w_out).astype(BF16)
    if small:
        up_layer = scatter_near(up_block, *up_far, (context_grad,))
    if not small:
        out_sum = tn(context, seen_first)
    given = (joint, context_grad, context, lse, n_ten)
    half_back = attend_back(*given, 0, half)
    if small:
        up_total = three_sum((after(up_layer[0], half_back[0]), *up_layer[1:]))
        half_back = (after(half_back[0], up_total), half_back[1])
    qkv_low, bias_sums = attend_back(*given, half, n_ten, half_back)
    if small:
        up_part = member_sum(up_total)
        encoded = after(encoded, up_part)
    encoded = swap(encoded)
    input_grad = summed_rows(qkv_low, w_qkv, nn) + first_grad
    input_grad = swap(input_grad.astype(BF16)).astype(F32)

    def core_halves(part):
        keep = lax.dynamic_slice_in_dim(part, core * slab, slab, axis=1)
        came = to_other(lax.dynamic_slice_in_dim(part, (1 - core) * slab, slab, axis=1))
        return jnp.stack(
            (jnp.where(core == 0, keep, came), jnp.where(core == 0, came, keep)), axis=0
        ).astype(F32)

    def scattered(total):
        rows = total.shape[0] // n_ten
        blocks = (
            total.astype(BF16)
            .reshape(n_ten, rows, n_chip, 2 * slab)
            .transpose(2, 0, 1, 3)
            .reshape(n_chip * n_ten, rows, 2 * slab)
        )
        return lax.psum_scatter(blocks, CHIPS, scatter_dimension=0, tiled=False)

    wide = (
        mid_gain_part,
        mid_shift_part,
        out_bias_part,
        end_gain_part,
        end_shift_part,
        down_bias_part,
    )
    narrow = (bias_sums[:, 0], bias_sums[:, 1], up_bias_part)
    if small:
        tail = []
        for vector in wide:
            tail.append(vector.reshape(n_chip, 2, n_ten, -1).transpose(0, 2, 1, 3))
        for vector in narrow:
            tail.append(vector.reshape(n_chip, n_ten, 1, -1))
        tail = [t.reshape(n_chip * n_ten, -1) for t in tail]
        tail_sizes = [t.shape[1] for t in tail]
        used = sum(tail_sizes)
        lines = -(-used // (2 * slab))
        lines = -(-lines // 16) * 16
        extra = jnp.concatenate(
            tail + [jnp.zeros((n_chip * n_ten, lines * 2 * slab - used), F32)], axis=1
        )
        extra = extra.reshape(n_chip, n_ten * lines, 2 * slab).astype(BF16)
        out_block = beside(context, seen_first)

        def last_block(move):
            owner = lax.bitwise_xor(chip, move)
            mark = lax.dynamic_index_in_dim(extra, owner, 0, keepdims=False)
            return jnp.concatenate(
                (beside(qkv_low, seen)(move), out_block(move), mark), axis=0
            )

        last = scatter_near(last_block, *scatter_far(last_block, (down_rows,)), (up_part,))
        last = three_sum((after(last[0], input_grad, encoded), *last[1:]))
        n_qkv = 3 * n_ten * cols
        n_out = n_ten * cols
        last = jnp.concatenate(
            (
                last[:n_qkv].reshape(n_ten, 3 * cols, 2 * slab),
                last[n_qkv : n_qkv + n_out].reshape(n_ten, cols, 2 * slab),
                last[n_qkv + n_out :].reshape(n_ten, lines, 2 * slab),
            ),
            axis=1,
        )
        down_cut = lambda move: lax.dynamic_slice_in_dim(
            down_rows, lax.bitwise_xor(chip, move) * (2 * slab), 2 * slab, axis=1
        )
        down_part = three_sum([down_cut(0)] + [to_chip(down_cut(move), move) for move in (1, 2, 3)])
        last_part = member_sum(last)
        vector_line = last_part[4 * cols :].reshape(-1).astype(F32)
        last_halves = core_halves(last_part[: 4 * cols])
        cut = [
            last_halves[:, : 3 * cols],
            last_halves[:, 3 * cols :],
            core_halves(up_part),
            core_halves(down_part),
        ]
    else:
        qkv_sum = tn(qkv_low, seen)
        parts = jnp.concatenate([scattered(t) for t in (qkv_sum, out_sum, up_sum, down_sum)], axis=0)
        halves = core_halves(parts)
        cut = [halves[:, bounds[i] : bounds[i + 1]] for i in range(4)]
    qkv_out = (
        cut[0].reshape(2, 3, cols, slab).transpose(3, 1, 0, 2).reshape(slab, 3, 2 * cols)
    )
    out_out = cut[1].reshape(2 * cols, slab)
    up_out = cut[2].reshape(2 * units, slab).T
    down_out = cut[3].reshape(2 * units, slab)

    if small:
        n_wide = sum(tail_sizes[:6])
        doubled = vector_line[:n_wide].reshape(6, 2, -1)
        own = lax.dynamic_index_in_dim(doubled, core, 1, keepdims=False)
        away = to_other(lax.dynamic_index_in_dim(doubled, 1 - core, 1, keepdims=False))
        own = own + away
        rest = vector_line[n_wide:]
        n_q, n_v, n_up = tail_sizes[6:]
        grads = [own[i] for i in range(6)] + [
            rest[:n_q],
            rest[n_q : n_q + n_v],
            rest[n_q + n_v : n_q + n_v + n_up],
        ]
    else:

        def placed(vector):
            blank = jnp.zeros((n_ten, 2, vector.size // n_ten), F32)
            return lax.dynamic_update_slice_in_dim(
                blank, vector.reshape(n_ten, 1, -1), core, 1
            ).reshape(-1)

        flat = list(wide) + [placed(v) for v in narrow]
        devices = n_chip * 2 * n_ten
        flat = [v.reshape(devices, -1) for v in flat]
        sums = lax.psum_scatter(
            jnp.concatenate(flat, axis=1), ALL, scatter_dimension=0, tiled=False
        )
        grads = []
        at = 0
        for v in flat:
            grads.append(sums[at : at + v.shape[1]])
            at += v.shape[1]
    g_mid_gain, g_mid_shift, g_out_bias, g_end_gain, g_end_shift, g_down_bias, g_q, g_v, g_up = (
        grads
    )
    return (
        encoded,
        input_grad,
        qkv_out,
        out_out,
        up_out,
        down_out,
        g_mid_gain,
        g_mid_shift,
        g_q,
        g_v,
        g_out_bias,
        g_end_gain,
        g_end_shift,
        g_up,
        g_down_bias,
    )


def solution(mesh):
    n_dp, n_ten = mesh.devices.shape
    inner = Mesh(mesh.devices.reshape(n_dp // 2, 2, n_ten), ALL)
    rows = P(ALL, None)
    vector = P(ALL)
    dp = ("chip", "core")
    weights = (P(dp, None, "tensor"), P("tensor", dp), P(dp, "tensor"), P("tensor", dp))
    return jax.shard_map(
        on_device,
        mesh=inner,
        in_specs=(rows, *weights, *(vector,) * 9, rows),
        out_specs=(rows, rows, *weights, *(vector,) * 9),
        check_vma=False,
    )
```

```python
import functools

import jax
import jax.numpy as jnp
from jax import lax
from jax.experimental import pallas as pl
from jax.experimental.pallas import tpu as pltpu
from jax.sharding import Mesh
from jax.sharding import PartitionSpec as P

HD = 64
LEN = 1024
PAIR = 2 * HD
QB = 1024
VMEM = 56 * 1024 * 1024
ALL = ("chip", "core", "tensor")
CHIPS = ("chip", "tensor")
F32 = jnp.float32
BF16 = jnp.bfloat16
SCALE = HD ** (-0.5)
EPS = 1e-05


def nt(left, right):
    return lax.dot_general(left, right, (((1,), (1,)), ((), ())), preferred_element_type=F32)


def nn(left, right):
    return lax.dot_general(left, right, (((1,), (0,)), ((), ())), preferred_element_type=F32)


def tn(left, right):
    return lax.dot_general(left, right, (((0,), (0,)), ((), ())), preferred_element_type=F32)


def head_lane(rows, head):
    lane = lax.broadcasted_iota(jnp.int32, (rows, PAIR), 1)
    return (lane >= head * HD) & (lane < (head + 1) * HD)


def attend_kernel(q_ref, k_ref, v_ref, o_ref, lse_ref):
    rows = q_ref.shape[0]
    keys = k_ref[...]
    values_t = v_ref[...].astype(F32).T
    sub = lax.broadcasted_iota(jnp.int32, values_t.shape, 0)
    values_h = [
        jnp.where((sub >= h * HD) & (sub < (h + 1) * HD), values_t, 1.0).astype(BF16)
        for h in range(2)
    ]

    def block(step, carry):
        at = pl.ds(pl.multiple_of(step * QB, QB), QB)
        q = q_ref[at, :].astype(F32) * SCALE
        parts = []
        for h in range(2):
            qm = jnp.where(head_lane(QB, h), q, 0.0).astype(BF16)
            scores = nt(keys, qm)
            largest = jnp.max(scores, axis=0, keepdims=True)
            weights = jnp.exp(scores - largest).astype(BF16)
            out = nn(values_h[h], weights)
            total = out[(1 - h) * HD : (1 - h) * HD + 1, :]
            parts.append(out[h * HD : (h + 1) * HD, :] / total)
            lse_ref[0, h : h + 1, at] = largest + jnp.log(total)
        o_ref[at, :] = jnp.concatenate(parts, axis=0).T.astype(BF16)
        return carry

    lax.fori_loop(0, rows // QB, block, 0)


def without(count, kernel):
    def call(*refs):
        return kernel(*refs[count:])

    return call


def attend(joint, groups, first, last, so_far=()):
    rows = joint.shape[0]
    part = lambda c: pl.BlockSpec((rows, PAIR), lambda z: (0, 3 * (z + first) + c))
    kept = len(so_far)
    return pl.pallas_call(
        without(kept, attend_kernel),
        grid=(last - first,),
        in_specs=[pl.BlockSpec(memory_space=pl.ANY)] * kept + [part(0), part(1), part(2)],
        input_output_aliases={i: i for i in range(kept)},
        out_specs=[
            pl.BlockSpec((rows, PAIR), lambda z: (0, z + first)),
            pl.BlockSpec((1, 2, rows), lambda z: (z + first, 0, 0)),
        ],
        out_shape=[
            jax.ShapeDtypeStruct((rows, groups * PAIR), BF16),
            jax.ShapeDtypeStruct((groups, 2, rows), F32),
        ],
        compiler_params=pltpu.CompilerParams(vmem_limit_bytes=VMEM),
        cost_estimate=pl.CostEstimate(
            flops=(last - first) * 2 * rows * HD,
            bytes_accessed=(last - first) * rows,
            transcendentals=(last - first) * 2 * rows,
        ),
        name="attend",
    )(*so_far, joint, joint, joint)


def attend_back_kernel(q_ref, k_ref, v_ref, g_ref, o_ref, lse_ref, d_ref, sum_ref, dk_ref, dv_ref):
    rows = q_ref.shape[0]
    keys = k_ref[...]
    values = v_ref[...]
    keys_t = keys.astype(F32).T
    sub = lax.broadcasted_iota(jnp.int32, keys_t.shape, 0)
    keys_h = [
        jnp.where((sub >= h * HD) & (sub < (h + 1) * HD), keys_t, 0.0).astype(BF16)
        for h in range(2)
    ]
    dk_ref[...] = jnp.zeros_like(dk_ref)
    dv_ref[...] = jnp.zeros_like(dv_ref)

    def block(step, query_sum):
        at = pl.ds(pl.multiple_of(step * QB, QB), QB)
        q = q_ref[at, :].astype(F32) * SCALE
        g = g_ref[at, :].astype(F32)
        inner = (g * o_ref[at, :].astype(F32)).T
        dq = None
        for h in range(2):
            here = head_lane(QB, h)
            qm = jnp.where(here, q, 0.0).astype(BF16)
            gm = jnp.where(here, g, 0.0).astype(BF16)
            delta = jnp.sum(inner[h * HD : (h + 1) * HD, :], axis=0, keepdims=True)
            probs = jnp.exp(nt(keys, qm) - lse_ref[0, h : h + 1, at])
            score_grad = (probs * (nt(values, gm) - delta)).astype(BF16)
            dv_ref[...] += nn(probs.astype(BF16), gm)
            dk_ref[...] += nn(score_grad, qm)
            part = nn(keys_h[h], score_grad)
            dq = part if dq is None else dq + part
        dq = (dq.T * SCALE).astype(BF16)
        d_ref[at, 0:PAIR] = dq
        return query_sum + jnp.sum(dq.astype(F32), axis=0, keepdims=True)

    query_sum = lax.fori_loop(0, rows // QB, block, jnp.zeros((1, PAIR), F32))
    dv = dv_ref[...].astype(BF16)
    d_ref[:, PAIR : 2 * PAIR] = dk_ref[...].astype(BF16)
    d_ref[:, 2 * PAIR :] = dv
    sum_ref[0, 0:1, :] = query_sum
    sum_ref[0, 1:2, :] = jnp.sum(dv.astype(F32), axis=0, keepdims=True)


def attend_back(joint, context_grad, context, lse, groups, first, last, so_far=()):
    rows = joint.shape[0]
    part = lambda c: pl.BlockSpec((rows, PAIR), lambda z: (0, 3 * (z + first) + c))
    one = pl.BlockSpec((rows, PAIR), lambda z: (0, z + first))
    kept = len(so_far)
    return pl.pallas_call(
        without(kept, attend_back_kernel),
        grid=(last - first,),
        input_output_aliases={i: i for i in range(kept)},
        in_specs=[pl.BlockSpec(memory_space=pl.ANY)] * kept
        + [
            part(0),
            part(1),
            part(2),
            one,
            one,
            pl.BlockSpec((1, 2, rows), lambda z: (z + first, 0, 0)),
        ],
        out_specs=[
            pl.BlockSpec((rows, 3 * PAIR), lambda z: (0, z + first)),
            pl.BlockSpec((1, 2, PAIR), lambda z: (z + first, 0, 0)),
        ],
        out_shape=[
            jax.ShapeDtypeStruct((rows, 3 * groups * PAIR), BF16),
            jax.ShapeDtypeStruct((groups, 2, PAIR), F32),
        ],
        scratch_shapes=[pltpu.VMEM((rows, PAIR), F32), pltpu.VMEM((rows, PAIR), F32)],
        compiler_params=pltpu.CompilerParams(vmem_limit_bytes=VMEM),
        cost_estimate=pl.CostEstimate(
            flops=(last - first) * 2 * rows * HD,
            bytes_accessed=(last - first) * rows,
            transcendentals=(last - first) * 2 * rows,
        ),
        name="attend_back",
    )(*so_far, joint, joint, joint, context_grad, context, lse)


def normalized(values_in):
    average = jnp.mean(values_in, axis=-1, keepdims=True)
    centred = values_in - average
    inverse = lax.rsqrt(jnp.mean(centred * centred, axis=-1, keepdims=True) + EPS)
    return centred * inverse, inverse


def norm_back(grad, unit, inverse, gain):
    gain_part = jnp.sum(grad * unit, axis=0)
    shift_part = jnp.sum(grad, axis=0)
    u = grad * gain
    back = inverse * (
        u
        - jnp.mean(u, axis=-1, keepdims=True)
        - unit * jnp.mean(u * unit, axis=-1, keepdims=True)
    )
    return back, gain_part, shift_part, jnp.sum(back, axis=0)


def gelu_pair(x):
    phi = 0.5 * (1.0 + lax.erf(x * (0.5**0.5)))
    slope = phi + x * jnp.exp(-0.5 * x * x) * (0.5 / jnp.pi) ** 0.5
    return (x * phi).astype(BF16), slope.astype(BF16)


def to_other(value):
    return lax.ppermute(value, "core", [(0, 1), (1, 0)])


def both_rows(value):
    return jnp.concatenate((value, to_other(value)), axis=0)


def summed_rows(rows, weight, dot, ready=()):
    half = rows.shape[0] // 2
    away = to_other(after(dot(rows[half:], weight).astype(BF16), *ready))
    return dot(rows[:half], weight) + away.astype(F32)


def assemble_kernel(n_far, chip_ref, own_ref, x_ref, y_ref, *refs):
    far_refs, out_refs = refs[:n_far], refs[n_far:]
    chip = chip_ref[0]
    wide = own_ref.shape[2]
    lower = pl.program_id(0) < pl.num_programs(0) // 2
    start = 0
    for out_ref in out_refs:
        rows = slice(start, start + out_ref.shape[1])
        start += out_ref.shape[1]

        def columns(move):
            at = pl.multiple_of(lax.bitwise_xor(chip, move) * wide, wide)
            return pl.ds(at, wide)

        out_ref[0, :, columns(0)] = own_ref[0, rows, :]
        out_ref[0, :, columns(1)] = x_ref[0, rows, :]
        out_ref[0, :, columns(2)] = y_ref[0, rows, :]
        far = far_refs[0][0, rows, :]
        if n_far == 2:
            far = jnp.where(lower, far, far_refs[1][0, rows, :])
        out_ref[0, :, columns(3)] = far


def assemble(chip, blocks, heights):
    own, low = blocks[0], blocks[3]
    members, rows, wide = own.shape
    half = low.shape[0]
    one = pl.BlockSpec((1, rows, wide), lambda z, c: (z, 0, 0))
    far = [pl.BlockSpec((1, rows, wide), lambda z, c: (jnp.minimum(z, half - 1), 0, 0))]
    if len(blocks) == 5:
        far.append(pl.BlockSpec((1, rows, wide), lambda z, c: (jnp.maximum(z - half, 0), 0, 0)))
    return pl.pallas_call(
        functools.partial(assemble_kernel, len(far)),
        grid_spec=pltpu.PrefetchScalarGridSpec(
            num_scalar_prefetch=1,
            grid=(members,),
            in_specs=[one, one, one, *far],
            out_specs=[pl.BlockSpec((1, h, 4 * wide), lambda z, c: (z, 0, 0)) for h in heights],
        ),
        out_shape=[jax.ShapeDtypeStruct((members, h, 4 * wide), BF16) for h in heights],
        compiler_params=pltpu.CompilerParams(vmem_limit_bytes=VMEM),
        cost_estimate=pl.CostEstimate(
            flops=0, bytes_accessed=members * rows, transcendentals=0
        ),
        name="assemble",
    )(chip.reshape(1), *blocks)


def to_chip(value, move):
    return lax.ppermute(value, "chip", [(i, i ^ move) for i in range(4)])


def after(value, *earlier):
    return lax.optimization_barrier((value, *earlier))[0]


def layer_near(part, ready=()):
    own = after(lax.all_gather(part, "tensor", axis=0, tiled=False), *ready)
    return own, to_chip(own, 1), to_chip(own, 2)


def layer_far(by_x, by_y):
    half = by_x.shape[0] // 2
    return to_chip(by_y[:half], 1), to_chip(by_x[half:], 2)


def scatter_far(block, ready=()):
    far = block(3)
    half = far.shape[0] // 2
    return to_chip(after(far[:half], *ready), 1), to_chip(after(far[half:], *ready), 2)


def scatter_near(block, low, high, ready=()):
    half = low.shape[0]
    near_x = block(1)
    near_y = block(2)
    add = lambda a, b: (a.astype(F32) + b.astype(F32)).astype(BF16)
    near_y = jnp.concatenate((add(near_y[:half], low), near_y[half:]), axis=0)
    near_x = jnp.concatenate((near_x[:half], add(near_x[half:], high)), axis=0)
    near_x = after(near_x, *ready)
    near_y = after(near_y, *ready)
    return block(0), to_chip(near_x, 1), to_chip(near_y, 2)


def three_sum(parts):
    return sum(p.astype(F32) for p in parts).astype(BF16)


def in_chip_order(chip, blocks):
    b0, b1, b2, b3 = blocks
    odd_x = (chip & 1) == 1
    odd_y = (chip & 2) == 2
    a0, a1 = jnp.where(odd_x, b1, b0), jnp.where(odd_x, b0, b1)
    a2, a3 = jnp.where(odd_x, b3, b2), jnp.where(odd_x, b2, b3)
    return jnp.stack(
        (
            jnp.where(odd_y, a2, a0),
            jnp.where(odd_y, a3, a1),
            jnp.where(odd_y, a0, a2),
            jnp.where(odd_y, a1, a3),
        )
    )


def on_device(
    tokens,
    qkv_weight,
    out_weight,
    up_weight,
    down_weight,
    mid_gain,
    mid_shift,
    query_bias,
    value_bias,
    out_bias,
    end_gain,
    end_shift,
    up_bias,
    down_bias,
    cotangent,
):
    core = lax.axis_index("core")
    chip = lax.axis_index("chip")
    n_chip = lax.axis_size("chip")
    n_ten = lax.axis_size("tensor")
    strip = tokens.shape[0]
    width = tokens.shape[1]
    slab = qkv_weight.shape[0]
    cols = qkv_weight.shape[2] // 2
    units = up_weight.shape[1] // 2
    assert 2 * strip == LEN and cols == PAIR

    pairs = []
    for z in range(n_ten):
        pairs.append((z, z) if z % 2 == 0 else (z, n_ten + z - 1))
        pairs.append((n_ten + z, z + 1) if z % 2 == 0 else (n_ten + z, n_ten + z))
    swap = lambda value: lax.ppermute(value, ("core", "tensor"), pairs)

    vectors = (
        mid_gain,
        mid_shift,
        query_bias,
        value_bias,
        out_bias,
        end_gain,
        end_shift,
        up_bias,
        down_bias,
    )
    stack = jnp.concatenate(
        (
            jnp.moveaxis(qkv_weight.reshape(slab, 3, 2, cols), 0, 3)
            .transpose(1, 0, 2, 3)
            .reshape(2, 3 * cols, slab),
            out_weight.reshape(2, cols, slab),
            up_weight.T.reshape(2, units, slab),
            down_weight.reshape(2, units, slab),
        ),
        axis=1,
    )
    keep = lax.dynamic_index_in_dim(stack, core, 0, keepdims=False)
    came = to_other(lax.dynamic_index_in_dim(stack, 1 - core, 0, keepdims=False))
    shard = jnp.concatenate(
        (jnp.where(core == 0, keep, came), jnp.where(core == 0, came, keep)), axis=1
    )
    bounds = (0, 3 * cols, 4 * cols, 4 * cols + units, 4 * cols + 2 * units)

    mine = swap(tokens)
    seen = both_rows(mine)
    sizes = [v.shape[0] for v in vectors]
    n_vec = sum(sizes)
    flat = jnp.concatenate(vectors)
    small = n_chip == 4 and n_ten == 4
    if small:
        coarse = lax.reduce_precision(flat, 8, 7)
        middle_bits = lax.reduce_precision(flat - coarse, 8, 7)
        thirds = jnp.concatenate((coarse, middle_bits, flat - coarse - middle_bits)).astype(BF16)
        came = to_other(thirds)
        both = jnp.concatenate(
            (jnp.where(core == 0, thirds, came), jnp.where(core == 0, came, thirds))
        )
        lines = -(-both.size // (16 * 2 * slab)) * 16
        both = jnp.concatenate((both, jnp.zeros((lines * 2 * slab - both.size,), BF16)))
        first = jnp.concatenate((shard[: bounds[1]], both.reshape(lines, 2 * slab)), axis=0)
        third = shard[bounds[3] :][None]
        third = (third, *(to_chip(third, move) for move in (1, 2, 3)))
        blocks = layer_near(first, (mine, *third[1:]))
        blocks += layer_far(*blocks[1:])
        (w_qkv,) = assemble(chip, blocks, (3 * cols,))
        tails = [b[:, 3 * cols :] for b in blocks]
        tails = tails[:3] + [jnp.concatenate(tails[3:], axis=0)]
        packed = in_chip_order(chip, tails).reshape(n_chip, n_ten, -1)[:, :, : 6 * n_vec]
        packed = packed.reshape(n_chip, n_ten, 2, 3, n_vec).astype(F32)
        packed = packed[:, :, :, 0] + packed[:, :, :, 1] + packed[:, :, :, 2]
        packed = packed.transpose(0, 2, 1, 3).reshape(-1, n_vec)
        second = after(shard[bounds[1] : bounds[3]], blocks[0])
        mid_blocks = layer_near(second)
        (third,) = assemble(chip, third, (units,))
        w_down = lax.all_gather(after(third[0], blocks[1]), "tensor", axis=0, tiled=True)
        w_qkv = w_qkv.reshape(-1, width)
    else:

        def gathered(index):
            part = shard[bounds[index] : bounds[index + 1]]
            rows = part.shape[0]
            full = lax.all_gather(part, CHIPS, axis=0, tiled=False)
            return (
                full.reshape(n_chip, n_ten, rows, 2 * slab)
                .transpose(1, 2, 0, 3)
                .reshape(n_ten * rows, width)
            )

        w_qkv, w_out, w_up, w_down = (gathered(i) for i in range(4))
        packed = lax.all_gather(flat, ALL, axis=0, tiled=False)
    starts = [sum(sizes[:i]) for i in range(len(sizes))]
    whole = [packed[:, s : s + n].reshape(-1) for s, n in zip(starts, sizes)]
    gain_mid, shift_mid, bias_q, bias_v, bias_out, gain_end, shift_end, bias_up, bias_down = whole

    def own_half(vector):
        return lax.dynamic_index_in_dim(vector.reshape(n_ten, 2, -1), core, 1, keepdims=False)

    bias_q, bias_v, bias_up = own_half(bias_q), own_half(bias_v), own_half(bias_up)
    bias_qkv = jnp.stack((bias_q, jnp.zeros_like(bias_q), bias_v), axis=1).reshape(-1)
    bias_up = bias_up.reshape(-1)

    joint = (nt(seen, w_qkv) + bias_qkv).astype(BF16)
    half = n_ten // 2
    context, lse = attend(joint, n_ten, 0, half)
    if small:
        far = layer_far(*(after(block, context) for block in mid_blocks[1:]))
        context = after(context, *mid_blocks[1:])
    context, lse = attend(joint, n_ten, half, n_ten, (context, lse))
    if small:
        w_out, w_up = assemble(chip, (after(mid_blocks[0], context), *mid_blocks[1:], *far), (cols, units))
        w_out, w_up = w_out.reshape(-1, width), w_up.reshape(-1, width)
    branch = summed_rows(context, w_out, nn)
    unit_mid, inverse_mid = normalized(mine.astype(F32) + branch + bias_out)
    middle = unit_mid * gain_mid + shift_mid
    seen_middle = both_rows(middle.astype(BF16))
    hidden, slope = gelu_pair(nt(seen_middle, w_up) + bias_up)
    cot = swap(after(cotangent, w_down, hidden))
    branch_two = summed_rows(hidden, w_down, nn)
    unit_end, inverse_end = normalized(middle + branch_two + bias_down)
    encoded = (unit_end * gain_end + shift_end).astype(BF16)

    second_grad, end_gain_part, end_shift_part, down_bias_part = norm_back(
        cot.astype(F32), unit_end, inverse_end, gain_end
    )
    seen_second = both_rows(second_grad.astype(BF16))
    pre_grad = (nt(seen_second, w_down) * slope.astype(F32)).astype(BF16)
    up_bias_part = jnp.sum(pre_grad.astype(F32), axis=0)
    middle_grad = summed_rows(pre_grad, w_up, nn) + second_grad

    def member_sum(total):
        total = total.reshape(n_ten, -1, 2 * slab)
        return lax.psum_scatter(total, "tensor", scatter_dimension=0, tiled=False)

    def beside(rows, columns):
        def block(move):
            at = lax.bitwise_xor(chip, move) * (2 * slab)
            return tn(rows, lax.dynamic_slice_in_dim(columns, at, 2 * slab, axis=1)).astype(BF16)

        return block

    if small:
        down_sum = tn(hidden, seen_second).astype(BF16)
        down_rows = lax.psum_scatter(
            down_sum.reshape(n_ten, units, width), "tensor", scatter_dimension=0, tiled=False
        )
        up_block = beside(pre_grad, after(seen_middle, down_sum))
        up_far = scatter_far(up_block)
    else:
        down_sum = tn(hidden, seen_second)
        up_sum = tn(pre_grad, seen_middle)
    first_grad, mid_gain_part, mid_shift_part, out_bias_part = norm_back(
        middle_grad, unit_mid, inverse_mid, gain_mid
    )
    seen_first = both_rows(first_grad.astype(BF16))
    context_grad = nt(seen_first, w_out).astype(BF16)
    if small:
        up_layer = scatter_near(up_block, *up_far, (context_grad,))
    if not small:
        out_sum = tn(context, seen_first)
    given = (joint, context_grad, context, lse, n_ten)
    half_back = attend_back(*given, 0, half)
    if small:
        up_total = three_sum((after(up_layer[0], half_back[0]), *up_layer[1:]))
        half_back = (after(half_back[0], up_total), half_back[1])
    qkv_low, bias_sums = attend_back(*given, half, n_ten, half_back)
    if small:
        up_part = member_sum(up_total)
        encoded = after(encoded, up_part)
    encoded = swap(encoded)
    input_grad = summed_rows(qkv_low, w_qkv, nn) + first_grad
    input_grad = swap(after(input_grad.astype(BF16), encoded)).astype(F32)

    def core_halves(part):
        keep = lax.dynamic_slice_in_dim(part, core * slab, slab, axis=1)
        came = to_other(lax.dynamic_slice_in_dim(part, (1 - core) * slab, slab, axis=1))
        return jnp.stack(
            (jnp.where(core == 0, keep, came), jnp.where(core == 0, came, keep)), axis=0
        ).astype(F32)

    def scattered(total):
        rows = total.shape[0] // n_ten
        blocks = (
            total.astype(BF16)
            .reshape(n_ten, rows, n_chip, 2 * slab)
            .transpose(2, 0, 1, 3)
            .reshape(n_chip * n_ten, rows, 2 * slab)
        )
        return lax.psum_scatter(blocks, CHIPS, scatter_dimension=0, tiled=False)

    wide = (
        mid_gain_part,
        mid_shift_part,
        out_bias_part,
        end_gain_part,
        end_shift_part,
        down_bias_part,
    )
    narrow = (bias_sums[:, 0], bias_sums[:, 1], up_bias_part)
    if small:
        tail = []
        for vector in wide:
            tail.append(vector.reshape(n_chip, 2, n_ten, -1).transpose(0, 2, 1, 3))
        for vector in narrow:
            tail.append(vector.reshape(n_chip, n_ten, 1, -1))
        tail = [t.reshape(n_chip * n_ten, -1) for t in tail]
        tail_sizes = [t.shape[1] for t in tail]
        used = sum(tail_sizes)
        lines = -(-used // (2 * slab))
        lines = -(-lines // 16) * 16
        extra = jnp.concatenate(
            tail + [jnp.zeros((n_chip * n_ten, lines * 2 * slab - used), F32)], axis=1
        )
        extra = extra.reshape(n_chip, n_ten * lines, 2 * slab).astype(BF16)
        out_block = beside(context, seen_first)

        def last_block(move):
            owner = lax.bitwise_xor(chip, move)
            mark = lax.dynamic_index_in_dim(extra, owner, 0, keepdims=False)
            return jnp.concatenate(
                (beside(qkv_low, seen)(move), out_block(move), mark), axis=0
            )

        last = scatter_near(last_block, *scatter_far(last_block, (down_rows,)), (up_part,))
        last = three_sum((after(last[0], input_grad), *last[1:]))
        n_qkv = 3 * n_ten * cols
        n_out = n_ten * cols
        last = jnp.concatenate(
            (
                last[:n_qkv].reshape(n_ten, 3 * cols, 2 * slab),
                last[n_qkv : n_qkv + n_out].reshape(n_ten, cols, 2 * slab),
                last[n_qkv + n_out :].reshape(n_ten, lines, 2 * slab),
            ),
            axis=1,
        )
        down_cut = lambda move: lax.dynamic_slice_in_dim(
            down_rows, lax.bitwise_xor(chip, move) * (2 * slab), 2 * slab, axis=1
        )
        down_part = three_sum([down_cut(0)] + [to_chip(down_cut(move), move) for move in (1, 2, 3)])
        last_part = member_sum(last)
        vector_line = last_part[4 * cols :].reshape(-1).astype(F32)
        last_halves = core_halves(last_part[: 4 * cols])
        cut = [
            last_halves[:, : 3 * cols],
            last_halves[:, 3 * cols :],
            core_halves(up_part),
            core_halves(down_part),
        ]
    else:
        qkv_sum = tn(qkv_low, seen)
        parts = jnp.concatenate([scattered(t) for t in (qkv_sum, out_sum, up_sum, down_sum)], axis=0)
        halves = core_halves(parts)
        cut = [halves[:, bounds[i] : bounds[i + 1]] for i in range(4)]
    qkv_out = (
        cut[0].reshape(2, 3, cols, slab).transpose(3, 1, 0, 2).reshape(slab, 3, 2 * cols)
    )
    out_out = cut[1].reshape(2 * cols, slab)
    up_out = cut[2].reshape(2 * units, slab).T
    down_out = cut[3].reshape(2 * units, slab)

    if small:
        n_wide = sum(tail_sizes[:6])
        doubled = vector_line[:n_wide].reshape(6, 2, -1)
        own = lax.dynamic_index_in_dim(doubled, core, 1, keepdims=False)
        away = to_other(lax.dynamic_index_in_dim(doubled, 1 - core, 1, keepdims=False))
        own = own + away
        rest = vector_line[n_wide:]
        n_q, n_v, n_up = tail_sizes[6:]
        grads = [own[i] for i in range(6)] + [
            rest[:n_q],
            rest[n_q : n_q + n_v],
            rest[n_q + n_v : n_q + n_v + n_up],
        ]
    else:

        def placed(vector):
            blank = jnp.zeros((n_ten, 2, vector.size // n_ten), F32)
            return lax.dynamic_update_slice_in_dim(
                blank, vector.reshape(n_ten, 1, -1), core, 1
            ).reshape(-1)

        flat = list(wide) + [placed(v) for v in narrow]
        devices = n_chip * 2 * n_ten
        flat = [v.reshape(devices, -1) for v in flat]
        sums = lax.psum_scatter(
            jnp.concatenate(flat, axis=1), ALL, scatter_dimension=0, tiled=False
        )
        grads = []
        at = 0
        for v in flat:
            grads.append(sums[at : at + v.shape[1]])
            at += v.shape[1]
    g_mid_gain, g_mid_shift, g_out_bias, g_end_gain, g_end_shift, g_down_bias, g_q, g_v, g_up = (
        grads
    )
    return (
        encoded,
        input_grad,
        qkv_out,
        out_out,
        up_out,
        down_out,
        g_mid_gain,
        g_mid_shift,
        g_q,
        g_v,
        g_out_bias,
        g_end_gain,
        g_end_shift,
        g_up,
        g_down_bias,
    )


def solution(mesh):
    n_dp, n_ten = mesh.devices.shape
    inner = Mesh(mesh.devices.reshape(n_dp // 2, 2, n_ten), ALL)
    rows = P(ALL, None)
    vector = P(ALL)
    dp = ("chip", "core")
    weights = (P(dp, None, "tensor"), P("tensor", dp), P(dp, "tensor"), P("tensor", dp))
    return jax.shard_map(
        on_device,
        mesh=inner,
        in_specs=(rows, *weights, *(vector,) * 9, rows),
        out_specs=(rows, rows, *weights, *(vector,) * 9),
        check_vma=False,
    )
```
